32 devices in a mesh: row: 8 (over z, y), col: 4 (over x, core).
Axes of the slice: x: 2, y: 2, z: 4, core: 2. Of those that a mesh axis runs over, the one named last changes fastest.
Arguments:
- x_tiles: bfloat16 [192, 512, 128], P('row', 'col'), may hold values from -1.328125 to 1.328125
- tile_pos: int32 [8, 96], P('row', 'col'), may hold values from 0 to 127, as said below
- panel_ids: int32 [4], replicated, may hold values from 0 to 15, as said below
Outputs:
- square_part: float32 [8192, 8192], P('row', 'col')
The draws below stay inside these ranges and needn't reach their ends.
Inputs may be any that keep to these rules, and one draw needn't show every extreme that they name: `tile_pos`: on each device the 24 positions are distinct and increasing. Split the device's 8 x 16 local blocks into squares of 4 x 4 blocks aligned to multiples of 4: one square (drawn) holds exactly 10 stored blocks and every other square exactly 2. `panel_ids`: the 4 panels are distinct, and one of them is the last panel.
All inputs are finite; a program needn't handle non-finite values.
Results may differ from the reference program's by a relative error of at most 0.0003.
Values may be sent and summed in bfloat16 or wider, within the bound.
No kernel may reach another device: no remote copies, remote signals or barrier semaphores. Data moves between devices by JAX's collectives and lax.ppermute only.
A program may use at most 64 MiB of HBM per device.

```python
import jax
import jax.numpy as jnp

BS = 128
LR = 8
PW = 4
SECTIONS = 4
QD = 10
QS = 2
NB = 64
LC = 16
SLOTS = 24
N_ROW = 8
N_COL = 4


def draw_tile_pos(key, part):
    qrows = LR // PW
    qcols = LC // PW
    squares = qrows * qcols
    cells = PW * PW

    def one_device(device):
        dev_key = jax.random.fold_in(jax.random.fold_in(key, 7001), device)
        key_win, key_perm = jax.random.split(dev_key)
        winner = jax.random.randint(key_win, (), 0, squares)
        index = jnp.arange(squares, dtype=jnp.int32)
        counts = jnp.where(index == winner, QD, QS).astype(jnp.int32)
        ranks = jax.vmap(lambda sub: jax.random.permutation(sub, cells))(jax.random.split(key_perm, squares))
        chosen = (ranks < counts[:, None]).reshape(qrows, qcols, PW, PW)
        chosen = chosen.transpose(0, 2, 1, 3).reshape(-1)
        return jnp.nonzero(chosen, size=SLOTS)[0].astype(jnp.int32)
    all_rows = jax.vmap(one_device)(jnp.arange(N_ROW * N_COL, dtype=jnp.int32))
    return all_rows.reshape(N_ROW, N_COL * SLOTS).astype(jnp.int32)


def draw_panel_ids(key, part):
    panels = NB // PW
    others = jax.random.permutation(jax.random.fold_in(key, 9103), panels - 1)[:SECTIONS - 1].astype(jnp.int32)
    picked = jnp.concatenate([others, jnp.full((1,), panels - 1, jnp.int32)])
    order = jax.random.permutation(jax.random.fold_in(key, 9107), SECTIONS)
    return picked[order].astype(jnp.int32)


def steps_of(own_key, dims, pieces, least, largest):
    factor_of = 1.0
    for axis_at, blocks in pieces:
        draws = jax.random.uniform(jax.random.fold_in(jax.random.fold_in(own_key, 6), axis_at), (blocks,), jnp.float32, least / len(pieces), largest / len(pieces))
        factor_of = factor_of * jnp.repeat(jnp.exp(draws), dims[axis_at] // blocks).reshape((-1,) + (1,) * (len(dims) - 1 - axis_at))
    return factor_of


def scatter_about(key, shape, spread, most, shards=(), kind=jnp.bfloat16):
    result = spread * jax.random.normal(key, shape, jnp.float32)
    if shards:
        result = result * steps_of(key, shape, shards, -0.22, 0.18)
    return jnp.clip(result, -most, most).astype(kind)


def setup_inputs(seed: int = 0) -> dict:
    streams_of = jax.random.split(jax.random.key(seed), 4)
    return {
        "x_tiles": scatter_about(streams_of[0], (N_ROW * SLOTS, N_COL * BS, BS), ((SECTIONS * PW * BS // 5) ** -0.25), 1.328125, ((0, 8), (1, 4))),
        "tile_pos": draw_tile_pos(jax.random.fold_in(streams_of[3], 71), 0),
        "panel_ids": draw_panel_ids(jax.random.fold_in(streams_of[3], 71), 0),
    }


def reference(x_tiles, tile_pos, panel_ids):
    tiles = x_tiles.reshape(N_ROW, SLOTS, N_COL, BS, BS).transpose(0, 2, 1, 3, 4).reshape(N_ROW * N_COL * SLOTS, BS, BS)
    positions = tile_pos.reshape(N_ROW, N_COL, SLOTS)
    row_base = (jnp.arange(N_ROW, dtype=jnp.int32) * LR)[:, None, None]
    col_base = (jnp.arange(N_COL, dtype=jnp.int32) * LC)[None, :, None]
    glob_rows = (row_base + positions // LC).reshape(-1).astype(jnp.int32)
    glob_cols = (col_base + positions % LC).reshape(-1).astype(jnp.int32)
    square_part = jnp.zeros((NB * BS, NB * BS), jnp.float32)
    for section in range(SECTIONS):
        first = (panel_ids[section] * PW).astype(jnp.int32)
        col_rel = glob_cols - first
        col_in = (col_rel >= 0) & (col_rel < PW)
        col_idx = jnp.where(col_in, col_rel, PW).astype(jnp.int32)
        column_blocks = jnp.zeros((NB, PW, BS, BS), x_tiles.dtype).at[glob_rows, col_idx].set(tiles, mode="drop")
        column_panel = column_blocks.transpose(0, 2, 1, 3).reshape(NB * BS, PW * BS)
        row_rel = glob_rows - first
        row_in = (row_rel >= 0) & (row_rel < PW)
        row_idx = jnp.where(row_in, row_rel, PW).astype(jnp.int32)
        row_blocks = jnp.zeros((PW, NB, BS, BS), x_tiles.dtype).at[row_idx, glob_cols].set(tiles, mode="drop")
        row_panel = row_blocks.transpose(0, 2, 1, 3).reshape(PW * BS, NB * BS)
        square_part = square_part + jnp.dot(column_panel, row_panel, preferred_element_type=jnp.float32)
    return square_part
```

```python
import functools

import jax
import jax.numpy as jnp
from jax import lax
from jax.experimental import pallas as pl
from jax.experimental.pallas import tpu as pltpu
from jax.sharding import PartitionSpec as P

LR = 8
PW = 4
SECTIONS = 4
QD = 10
QS = 2
NOTE = 16
AT_ONCE = 4


class Sizes:
    def __init__(self, rows, cols, slots, bs):
        self.rows, self.cols, self.slots, self.bs = rows, cols, slots, bs
        self.lc = LR * rows // cols
        panel_most = (self.lc // PW) * QS + (QD - QS)
        self.share = -(-panel_most // rows)
        self.near = -(-max(0, slots - rows * self.share) // self.share)
        self.held = SECTIONS * self.share
        self.depth = SECTIONS * PW

    def given(self, d):
        return self.share * (2 if d < self.near else 1)


def section_of(panels_ref, panel):
    found = jnp.int32(-1)
    for j in range(SECTIONS):
        found = jnp.where(panels_ref[j] == panel, jnp.int32(j), found)
    return found


def owned_by(panels_ref, row):
    count, first, last = jnp.int32(0), jnp.int32(-1), jnp.int32(0)
    for j in reversed(range(SECTIONS)):
        mine = panels_ref[j] // (LR // PW) == row
        last = jnp.where(mine & (count == 0), j, last)
        first = jnp.where(mine, j, first)
        count = count + mine.astype(jnp.int32)
    return count, first, last


def deal(sz, count, picked, e, i):
    i = jnp.where(picked, i + 1, i)
    full = i == jnp.where((count == 2) & (e < sz.near), 2 * sz.share, sz.share)
    return jnp.where(full, e + 1, e), jnp.where(full, 0, i)


def pack_kernel(sz, pos_ref, panels_ref, pos_row_ref, x_ref, *refs):
    outs, all_ref, src_ref = refs[: sz.rows], refs[sz.rows], refs[sz.rows + 1]
    row = lax.axis_index("row")
    count, _, _ = owned_by(panels_ref, row)
    bs, most = sz.bs, 2 * sz.share
    for e in range(sz.rows * most):
        src_ref[e] = 0

    def one(s, state):
        e, i = state
        panel = row * (LR // PW) + pos_ref[0, s] // (sz.lc * PW)
        picked = section_of(panels_ref, panel) >= 0

        @pl.when(picked)
        def _():
            src_ref[e * most + i] = s

        return deal(sz, count, picked, e, i)

    lax.fori_loop(0, sz.slots, one, (jnp.int32(0), jnp.int32(0)))
    note = jnp.broadcast_to(pos_row_ref[...].astype(jnp.float32), (NOTE, sz.slots)).astype(x_ref.dtype)
    for e in range(sz.rows):
        for i in range(sz.given(e)):
            outs[e][i * bs : (i + 1) * bs] = x_ref[src_ref[e * most + i]]
        outs[e][sz.given(e) * bs :, : sz.slots] = note
    for s in range(sz.slots):
        all_ref[s * bs : (s + 1) * bs] = x_ref[s]
    all_ref[sz.slots * bs :, : sz.slots] = note


def hold_kernel(sz, panels_ref, *refs):
    came, hold_ref, notes_ref = refs[: sz.rows], refs[sz.rows], refs[sz.rows + 1]
    row = lax.axis_index("row")
    n = sz.share * sz.bs
    for d in range(sz.rows):
        note = came[d][sz.given(d) * sz.bs :].astype(jnp.float32)[:1, : sz.slots]
        notes_ref[d : d + 1, :] = note.astype(jnp.int32)
    for j in range(SECTIONS):
        owner = panels_ref[j] // (LR // PW)
        _, first, _ = owned_by(panels_ref, owner)
        for d in range(sz.rows):

            @pl.when(((owner ^ row) == d) & (first == j))
            def _():
                hold_ref[j * n : (j + 1) * n] = came[d][:n]

            if d < sz.near:

                @pl.when(((owner ^ row) == d) & (first != j))
                def _():
                    hold_ref[j * n : (j + 1) * n] = came[d][n : 2 * n]


def column_meta_kernel(sz, notes_ref, panels_ref, b_list):
    row = lax.axis_index("row")

    def clear(i, _):
        b_list[i] = -1
        return 0

    lax.fori_loop(0, sz.rows * sz.held, clear, 0)

    def one_row(owner, _):
        count, first, last = owned_by(panels_ref, owner)

        def one(s, state):
            e, i = state
            pos = notes_ref[owner ^ row, s]
            local_row, local_col = pos // sz.lc, pos % sz.lc
            section = section_of(panels_ref, owner * (LR // PW) + local_row // PW)
            picked = section >= 0

            @pl.when(picked)
            def _():
                at = jnp.where(i < sz.share, first * sz.share + i, last * sz.share + i - sz.share)
                b_list[(owner ^ e ^ row) * sz.held + at] = (section * PW + local_row % PW) * sz.lc + local_col

            return deal(sz, count, picked, e, i)

        @pl.when(count > 0)
        def _():
            lax.fori_loop(0, sz.slots, one, (jnp.int32(0), jnp.int32(0)))

        return 0

    lax.fori_loop(0, sz.rows, one_row, 0)


def row_meta_kernel(sz, notes_ref, panels_ref, a_list):
    for i in range(LR):
        a_list[i * (sz.depth + 1)] = 0

    def one(t, _):
        owner, s = t // sz.slots, t % sz.slots
        pos = notes_ref[owner, s]
        local_row, local_col = pos // sz.lc, pos % sz.lc
        section = section_of(panels_ref, owner * (sz.lc // PW) + local_col // PW)

        @pl.when(section >= 0)
        def _():
            base = local_row * (sz.depth + 1)
            n = a_list[base] + 1
            a_list[base + n] = t * sz.depth + section * PW + local_col % PW
            a_list[base] = n

        return 0

    lax.fori_loop(0, sz.cols * sz.slots, one, 0)


def product_kernel(sz, a_list, b_list, a_ref, *refs):
    b_refs = refs[: sz.rows]
    out_ref, lhs, b_dense = refs[sz.rows :]
    bs, depth = sz.bs, sz.depth
    step = pl.program_id(0)

    @pl.when(step == 0)
    def _():
        b_dense[...] = jnp.zeros_like(b_dense)
        for e in range(sz.rows):
            for h in range(sz.held):
                at = b_list[e * sz.held + h]

                @pl.when(at >= 0)
                def _():
                    k, c = at // sz.lc, at % sz.lc
                    b_dense[k, :, pl.ds(pl.multiple_of(c * bs, bs), bs)] = b_refs[e][h * bs : (h + 1) * bs]

    base = step * (depth + 1)
    n = a_list[base]
    width = out_ref.shape[1]
    chunk = min(width, 512)

    def group(g, first):
        ks = []
        for u in range(AT_ONCE):
            t = g * AT_ONCE + u
            there = t < n
            code = jnp.where(there, a_list[base + 1 + jnp.minimum(t, depth - 1)], 0)
            place, k = code // depth, code % depth
            owner, s = place // sz.slots, place % sz.slots
            block = a_ref[owner, pl.ds(pl.multiple_of(s * bs, bs), bs), :]
            lhs[:, u * bs : (u + 1) * bs] = jnp.where(there, block, jnp.zeros_like(block))
            ks.append(k)
        for c in range(0, width, chunk):
            rhs = jnp.concatenate([b_dense[k, :, c : c + chunk] for k in ks], axis=0)
            part = jnp.dot(lhs[...], rhs, preferred_element_type=jnp.float32)
            if first:
                out_ref[:, c : c + chunk] = part
            else:
                out_ref[:, c : c + chunk] += part

    group(0, True)

    def more(g, _):
        group(g, False)
        return 0

    lax.fori_loop(1, (n + AT_ONCE - 1) // AT_ONCE, more, 0)


def flip(x, axis, d):
    return lax.ppermute(x, axis, [(i, i ^ d) for i in range(lax.axis_size(axis))])


def gather_by_flips(x, axis):
    n = lax.axis_size(axis)
    got, bit = {0: x}, n // 2
    while bit:
        for d in list(got):
            got[d | bit] = flip(got[d], axis, bit)
        bit //= 2
    return [got[d] for d in range(n)]


def per_device(x_tiles, tile_pos, panel_ids):
    rows, cols = lax.axis_size("row"), lax.axis_size("col")
    slots, bs, _ = x_tiles.shape
    dtype = x_tiles.dtype
    sz = Sizes(rows, cols, slots, bs)
    smem = pl.BlockSpec(memory_space=pltpu.SMEM)
    vmem = pl.BlockSpec(memory_space=pltpu.VMEM)

    *parts, mine = pl.pallas_call(
        functools.partial(pack_kernel, sz),
        out_shape=[jax.ShapeDtypeStruct((sz.given(d) * bs + NOTE, bs), dtype) for d in range(rows)]
        + [jax.ShapeDtypeStruct((slots * bs + NOTE, bs), dtype)],
        in_specs=[smem, smem, vmem, vmem],
        out_specs=[vmem] * (rows + 1),
        scratch_shapes=[pltpu.SMEM((rows * 2 * sz.share,), jnp.int32)],
    )(tile_pos, panel_ids, tile_pos, x_tiles)

    a_all = lax.all_gather(mine, "col")
    came = [parts[0]] + [flip(parts[d], "row", d) for d in range(1, rows)]
    hold, column_notes = pl.pallas_call(
        functools.partial(hold_kernel, sz),
        out_shape=[
            jax.ShapeDtypeStruct((sz.held * bs, bs), dtype),
            jax.ShapeDtypeStruct((rows, slots), jnp.int32),
        ],
        in_specs=[smem] + [vmem] * rows,
        out_specs=[vmem, vmem],
    )(panel_ids, *came)
    b_parts = gather_by_flips(hold, "row")

    b_list = pl.pallas_call(
        functools.partial(column_meta_kernel, sz),
        out_shape=jax.ShapeDtypeStruct((rows * sz.held,), jnp.int32),
        in_specs=[smem, smem],
        out_specs=smem,
    )(column_notes, panel_ids)
    a_list = pl.pallas_call(
        functools.partial(row_meta_kernel, sz),
        out_shape=jax.ShapeDtypeStruct((LR * (sz.depth + 1),), jnp.int32),
        in_specs=[smem, smem],
        out_specs=smem,
    )(a_all[:, -1, :slots].astype(jnp.int32), panel_ids)

    width = sz.lc * bs
    return pl.pallas_call(
        functools.partial(product_kernel, sz),
        out_shape=jax.ShapeDtypeStruct((LR * bs, width), jnp.float32),
        grid_spec=pltpu.PrefetchScalarGridSpec(
            num_scalar_prefetch=2,
            grid=(LR,),
            in_specs=[pl.BlockSpec((cols, slots * bs + NOTE, bs), lambda i, *_: (0, 0, 0))]
            + [pl.BlockSpec((sz.held * bs, bs), lambda i, *_: (0, 0))] * rows,
            out_specs=pl.BlockSpec((bs, width), lambda i, *_: (i, 0)),
            scratch_shapes=[
                pltpu.VMEM((bs, AT_ONCE * bs), dtype),
                pltpu.VMEM((sz.depth, bs, width), dtype),
            ],
        ),
        compiler_params=pltpu.CompilerParams(vmem_limit_bytes=40 * 2**20),
        cost_estimate=pl.CostEstimate(flops=2 * 10**9, bytes_accessed=12 * 2**20, transcendentals=0),
    )(a_list, b_list, a_all, *b_parts)


def solution(mesh):
    in_specs = (P("row", "col", None), P("row", "col"), P())
    out_specs = P("row", "col")
    return jax.shard_map(
        per_device, mesh=mesh, in_specs=in_specs, out_specs=out_specs, check_vma=False
    )
```

```python
import functools

import jax
import jax.numpy as jnp
from jax import lax
from jax.experimental import pallas as pl
from jax.experimental.pallas import tpu as pltpu
from jax.sharding import PartitionSpec as P

LR = 8
PW = 4
SECTIONS = 4
QD = 10
QS = 2
NOTE = 16
AT_ONCE = 8


class Sizes:
    def __init__(self, rows, cols, slots, bs):
        self.rows, self.cols, self.slots, self.bs = rows, cols, slots, bs
        self.lc = LR * rows // cols
        self.panels = rows * LR // PW
        panel_most = (self.lc // PW) * QS + (QD - QS)
        self.share = -(-panel_most // rows)
        self.near = -(-max(0, slots - rows * self.share) // self.share)
        self.held = SECTIONS * self.share
        self.depth = SECTIONS * PW
        self.late = [d * self.held + h for d in range(rows) if d & 1 and d & (rows // 2) for h in range(self.held)]

    def given(self, d):
        return self.share * (2 if d < self.near else 1)


def list_sections(sz, panels_ref, section_ref):
    for p in range(sz.panels):
        section_ref[p] = -1
    for j in range(SECTIONS):
        section_ref[panels_ref[j]] = j


def owned_by(panels_ref, row):
    count, first, last = jnp.int32(0), jnp.int32(-1), jnp.int32(0)
    for j in reversed(range(SECTIONS)):
        mine = lax.div(panels_ref[j], LR // PW) == row
        last = jnp.where(mine & (count == 0), j, last)
        first = jnp.where(mine, j, first)
        count = count + mine.astype(jnp.int32)
    return count, first, last


def deal(sz, count, picked, e, i):
    i = jnp.where(picked, i + 1, i)
    full = i == jnp.where((count == 2) & (e < sz.near), 2 * sz.share, sz.share)
    return jnp.where(full, e + 1, e), jnp.where(full, 0, i)


def pack_kernel(sz, pos_ref, panels_ref, pos_row_ref, x_ref, *refs):
    outs, (all_ref, section_ref, plan_ref, src_ref) = refs[: sz.rows], refs[sz.rows :]
    row = lax.axis_index("row")
    count, _, _ = owned_by(panels_ref, row)
    bs, most = sz.bs, 2 * sz.share
    for e in range(sz.rows * most):
        src_ref[e] = 0
    list_sections(sz, panels_ref, section_ref)
    for d in range(sz.rows):
        for i, value in enumerate(owned_by(panels_ref, row ^ d)):
            plan_ref[3 * d + i] = value

    def one(s, state):
        e, i = state
        picked = section_ref[row * (LR // PW) + lax.div(pos_ref[0, s], sz.lc * PW)] >= 0

        @pl.when(picked)
        def _():
            src_ref[e * most + i] = s

        return deal(sz, count, picked, e, i)

    lax.fori_loop(0, sz.slots, one, (jnp.int32(0), jnp.int32(0)))
    note = jnp.broadcast_to(pos_row_ref[...].astype(jnp.float32), (NOTE, sz.slots)).astype(x_ref.dtype)
    for e in range(sz.rows):
        for i in range(sz.given(e)):
            outs[e][i * bs : (i + 1) * bs] = x_ref[src_ref[e * most + i]]
        outs[e][sz.given(e) * bs :, : sz.slots] = note
    for s in range(sz.slots):
        all_ref[s * bs : (s + 1) * bs] = x_ref[s]
    all_ref[sz.slots * bs :, : sz.slots] = note


def hold_kernel(sz, plan_ref, *refs):
    came, hold_ref, notes_ref = refs[: sz.rows], refs[sz.rows], refs[sz.rows + 1]
    n = sz.share * sz.bs

    for d in range(sz.rows):
        note = came[d][sz.given(d) * sz.bs :].astype(jnp.float32)[:1, : sz.slots]
        notes_ref[d : d + 1, :] = note.astype(jnp.int32)
    for d in range(sz.rows):
        count, first, last = (plan_ref[3 * d + i] for i in range(3))

        @pl.when(count > 0)
        def _():
            hold_ref[pl.ds(pl.multiple_of(first * n, n), n)] = came[d][:n]

        if d < sz.near:

            @pl.when(count == 2)
            def _():
                hold_ref[pl.ds(pl.multiple_of(last * n, n), n)] = came[d][n : 2 * n]


def column_meta_kernel(sz, notes_ref, section_ref, plan_ref, b_list, b_dense):
    row = lax.axis_index("row")
    b_dense[...] = jnp.zeros_like(b_dense)

    for i in range(sz.rows * sz.held):
        b_list[i] = -1

    def one_row(d, _):
        count, first, last = (plan_ref[3 * d + i] for i in range(3))
        owner = row ^ d

        def one(s, state):
            e, i = state
            pos = notes_ref[d, s]
            local_row, local_col = lax.div(pos, sz.lc), lax.rem(pos, sz.lc)
            section = section_ref[owner * (LR // PW) + lax.div(local_row, PW)]
            picked = section >= 0

            @pl.when(picked)
            def _():
                at = jnp.where(i < sz.share, first * sz.share + i, last * sz.share + i - sz.share)
                b_list[(d ^ e) * sz.held + at] = (section * PW + lax.rem(local_row, PW)) * sz.lc + local_col

            return deal(sz, count, picked, e, i)

        @pl.when(count > 0)
        def _():
            lax.fori_loop(0, sz.slots, one, (jnp.int32(0), jnp.int32(0)))

        return 0

    lax.fori_loop(0, sz.rows, one_row, 0)


def row_meta_kernel(sz, notes_ref, section_ref, b_list, *refs):
    a_refs, (a_list, late_list, a_sorted, by_k, latest) = refs[: sz.cols], refs[sz.cols :]
    col = lax.axis_index("col")
    bs, depth = sz.bs, sz.depth
    for i in range(LR):
        a_list[i * (depth + 1)] = 0
    for k in range(depth):
        by_k[k * (LR + 1)] = 0

    for e in range(sz.cols):

        def one(s, _):
            pos = notes_ref[e, s]
            local_row, local_col = lax.div(pos, sz.lc), lax.rem(pos, sz.lc)
            section = section_ref[(e ^ col) * (sz.lc // PW) + lax.div(local_col, PW)]

            @pl.when(section >= 0)
            def _():
                k = section * PW + lax.rem(local_col, PW)
                base = local_row * (depth + 1)
                n = a_list[base]
                a_list[base + 1 + n] = k
                a_list[base] = n + 1
                place = local_row * depth + n
                base = k * (LR + 1)
                n = by_k[base]
                by_k[base + 1 + n] = place
                by_k[base] = n + 1
                a_sorted[place] = a_refs[e][pl.ds(pl.multiple_of(s * bs, bs), bs), :]

            return 0

        lax.fori_loop(0, sz.slots, one, 0)

    total = jnp.int32(0)
    for h, at_place in enumerate(sz.late):
        at = b_list[at_place]
        there = at >= 0
        at = jnp.maximum(at, 0)
        base, c = lax.div(at, sz.lc) * (LR + 1), lax.rem(at, sz.lc)
        n = jnp.where(there, by_k[base], 0)

        def pair(t, _):
            place = by_k[base + 1 + t]
            tile = lax.div(place, depth) * sz.lc + c
            late_list[2 + 2 * (total + t)] = h * (LR * depth) + place
            late_list[3 + 2 * (total + t)] = tile
            latest[tile] = total + t
            return 0

        lax.fori_loop(0, n, pair, 0)
        total = total + n

    def mark(t, tiles):
        tile = late_list[3 + 2 * t]
        last = (latest[tile] == t).astype(jnp.int32)
        late_list[3 + 2 * t] = 2 * tile + last
        return tiles + last

    late_list[0] = total
    late_list[1] = lax.fori_loop(0, total, mark, jnp.int32(0))


def tile(sz, i, c):
    return pl.ds(pl.multiple_of(i * sz.bs, sz.bs), sz.bs), pl.ds(pl.multiple_of(c * sz.bs, sz.bs), sz.bs)


def product_kernel(sz, starts, a_list, b_list, b_clear, a_sorted, *refs):
    b_refs, (total, out_ref, b_dense, sem) = refs[: len(starts)], refs[len(starts) :]
    bs, depth = sz.bs, sz.depth
    for start, b_ref in zip(starts, b_refs):
        for h in range(b_ref.shape[0] // bs):
            at = b_list[start + h]

            @pl.when(at >= 0)
            def _():
                k, c = lax.div(at, sz.lc), lax.rem(at, sz.lc)
                b_dense[k, :, pl.ds(pl.multiple_of(c * bs, bs), bs)] = b_ref[h * bs : (h + 1) * bs]

    width = total.shape[1]
    chunk = min(width, 512)

    def to_out(i):
        here = pl.ds(pl.multiple_of(i * bs, bs), bs)
        return pltpu.make_async_copy(total.at[here], out_ref.at[here], sem)

    def one_row(i, _):
        base = i * (depth + 1)
        n = a_list[base]
        here = pl.ds(pl.multiple_of(i * bs, bs), bs)

        def group(start, size, first):
            ks, blocks = [], []
            for t in range(size):
                at = jnp.minimum(start + t, depth - 1)
                there = start + t < n
                block = a_sorted[i * depth + at]
                blocks.append(jnp.where(there, block, jnp.zeros_like(block)))
                ks.append(jnp.where(there, a_list[base + 1 + at], 0))
            lhs = jnp.concatenate(blocks, axis=1)
            for c in range(0, width, chunk):
                rhs = jnp.concatenate([b_dense[k, :, c : c + chunk] for k in ks], axis=0)
                part = jnp.dot(lhs, rhs, preferred_element_type=jnp.float32)
                if first:
                    total[here, c : c + chunk] = part
                else:
                    total[here, c : c + chunk] += part

        @pl.when(n <= 2)
        def _():
            group(0, 2, True)

        @pl.when(n > 2)
        def _():
            group(0, 4, True)

        def more(g, _):
            group(4 + 2 * g, 2, False)
            return 0

        lax.fori_loop(0, lax.div(jnp.maximum(n - 3, 0), 2), more, 0)
        to_out(i).start()
        return 0

    lax.fori_loop(0, LR, one_row, 0)

    def done(i, _):
        to_out(i).wait()
        return 0

    lax.fori_loop(0, LR, done, 0)


def last_kernel(sz, late_list, total_in, out_in, a_sorted, *refs):
    b_refs, (total, out_ref, right, parts, sem) = refs[:-5], refs[-5:]
    bs, every = sz.bs, LR * sz.depth
    count = late_list[0]
    at = 0
    for b_ref in b_refs:
        for h in range(b_ref.shape[0] // bs):
            right[at] = b_ref[h * bs : (h + 1) * bs]
            at += 1

    def to_out(at):
        return pltpu.make_async_copy(total.at[at], out_ref.at[at], sem)

    def group(g, _):
        for u in range(AT_ONCE):
            code = late_list[2 + 2 * jnp.minimum(g * AT_ONCE + u, count - 1)]
            parts[u] = jnp.dot(
                a_sorted[lax.rem(code, every)], right[lax.div(code, every)], preferred_element_type=jnp.float32
            )
        for u in range(AT_ONCE):
            t = g * AT_ONCE + u

            @pl.when(t < count)
            def _():
                code = late_list[3 + 2 * t]
                at = tile(sz, lax.div(code, 2 * sz.lc), lax.rem(lax.div(code, 2), sz.lc))
                total[at] += parts[u]

                @pl.when(lax.rem(code, 2) == 1)
                def _():
                    to_out(at).start()

        return 0

    lax.fori_loop(0, lax.div(count + AT_ONCE - 1, AT_ONCE), group, 0)

    def done(t, _):
        to_out((slice(0, bs), slice(0, bs))).wait()
        return 0

    lax.fori_loop(0, late_list[1], done, 0)


def flip(x, axis, d):
    return lax.ppermute(x, axis, [(i, i ^ d) for i in range(lax.axis_size(axis))])


def gather_by_flips(x, axis):
    n = lax.axis_size(axis)
    got, bit = {0: x}, n // 2
    while bit:
        for d in list(got):
            got[d | bit] = flip(got[d], axis, bit)
        bit //= 2
    return [got[d] for d in range(n)]


def per_device(x_tiles, tile_pos, panel_ids):
    rows, cols = lax.axis_size("row"), lax.axis_size("col")
    slots, bs, _ = x_tiles.shape
    dtype = x_tiles.dtype
    sz = Sizes(rows, cols, slots, bs)
    smem = pl.BlockSpec(memory_space=pltpu.SMEM)
    vmem = pl.BlockSpec(memory_space=pltpu.VMEM)

    *parts, mine, sections, plan = pl.pallas_call(
        functools.partial(pack_kernel, sz),
        out_shape=[pltpu.VMEM((sz.given(d) * bs + NOTE, bs), dtype) for d in range(rows)]
        + [
            pltpu.VMEM((slots * bs + NOTE, bs), dtype),
            pltpu.SMEM((sz.panels,), jnp.int32),
            pltpu.SMEM((3 * rows,), jnp.int32),
        ],
        in_specs=[smem, smem, vmem, vmem],
        out_specs=[vmem] * (rows + 1) + [smem, smem],
        scratch_shapes=[pltpu.SMEM((rows * 2 * sz.share,), jnp.int32)],
    )(tile_pos, panel_ids, tile_pos, x_tiles)

    in_vmem = functools.partial(pltpu.with_memory_space_constraint, memory_space=pltpu.VMEM)
    in_smem = functools.partial(pltpu.with_memory_space_constraint, memory_space=pltpu.SMEM)
    sections, plan = in_smem(sections), in_smem(plan)
    a_got, a_bit = {0: mine}, cols // 2
    a_got[a_bit] = flip(mine, "col", a_bit)
    came = [parts[0]] + [flip(parts[d], "row", d) for d in range(1, rows)]
    hold, column_notes = pl.pallas_call(
        functools.partial(hold_kernel, sz),
        out_shape=[
            pltpu.VMEM((sz.held * bs, bs), dtype),
            jax.ShapeDtypeStruct((rows, slots), jnp.int32),
        ],
        in_specs=[smem] + [vmem] * rows,
        out_specs=[vmem, vmem],
    )(plan, *map(in_vmem, came))
    width = sz.lc * bs
    params = pltpu.CompilerParams(vmem_limit_bytes=32 * 2**20)
    b_list, b_clear = pl.pallas_call(
        functools.partial(column_meta_kernel, sz),
        out_shape=[
            pltpu.SMEM((rows * sz.held,), jnp.int32),
            pltpu.VMEM((sz.depth, bs, width), dtype),
        ],
        in_specs=[smem, smem, smem],
        out_specs=[smem, vmem],
        compiler_params=params,
    )(column_notes, sections, plan)

    bits = [1 << b for b in reversed(range(rows.bit_length() - 1))]
    a_got, hold_too = lax.optimization_barrier((a_got, hold))
    got = {0: [hold], **{bit: [flip(hold_too if bit < bits[0] else hold, "row", bit)] for bit in bits}}
    while a_bit:
        for d in list(a_got):
            if d | a_bit not in a_got:
                a_got[d | a_bit] = flip(a_got[d], "col", a_bit)
        a_bit //= 2
    a_parts = [a_got[d] for d in range(cols)]
    row_notes = jnp.stack([a[-1, :slots] for a in a_parts]).astype(jnp.int32)
    a_list, late_list, a_sorted = pl.pallas_call(
        functools.partial(row_meta_kernel, sz),
        out_shape=[
            pltpu.SMEM((LR * (sz.depth + 1),), jnp.int32),
            pltpu.SMEM((2 + 2 * len(sz.late) * LR,), jnp.int32),
            pltpu.VMEM((LR * sz.depth, bs, bs), dtype),
        ],
        in_specs=[smem] * 3 + [vmem] * cols,
        out_specs=[smem, smem, vmem],
        scratch_shapes=[
            pltpu.SMEM((sz.depth * (LR + 1),), jnp.int32),
            pltpu.SMEM((LR * sz.lc,), jnp.int32),
        ],
        compiler_params=params,
    )(row_notes, sections, in_smem(b_list), *map(in_vmem, a_parts))
    got[2], a_list, a_sorted = lax.optimization_barrier((got[2], a_list, a_sorted))
    if 3 not in got:
        got[3] = [flip(got[2][0], "row", 1)]
    (top, second), half = bits[:2], sz.held * bs // 2
    got[top], got[2], got[1], a_list, a_sorted = lax.optimization_barrier(
        (got[top], got[2], got[1], a_list, a_sorted)
    )
    first, rest = got[top][0][:half], got[top][0][half:]
    first, rest = flip(first, "row", second), flip(rest, "row", second)
    rest, got[3] = lax.optimization_barrier((rest, got[3]))
    got[top | second] = [first, rest]
    got[top | second | 1] = [flip(p, "row", 1) for p in got[top | second]]
    got[top | 1] = [flip(got[top][0][:half], "row", 1), flip(got[1][0][half:], "row", top)]
    for bit in bits[1:]:
        for d in list(got):
            if d | bit not in got:
                got[d | bit] = [flip(p, "row", bit) for p in got[d]]

    early, late = [], []
    for d in range(rows):
        for i, piece in enumerate(got[d]):
            if d * sz.held in sz.late:
                late.append(in_vmem(piece))
            else:
                early.append((d * sz.held + i * half // bs, in_vmem(piece)))

    total, out = pl.pallas_call(
        functools.partial(product_kernel, sz, [start for start, _ in early]),
        out_shape=[
            pltpu.VMEM((LR * bs, width), jnp.float32),
            jax.ShapeDtypeStruct((LR * bs, width), jnp.float32),
            pltpu.VMEM((sz.depth, bs, width), dtype),
        ],
        in_specs=[smem, smem] + [vmem] * (2 + len(early)),
        out_specs=[vmem, pl.BlockSpec(memory_space=pl.ANY), vmem],
        input_output_aliases={2: 2},
        scratch_shapes=[pltpu.SemaphoreType.DMA],
        compiler_params=params,
        cost_estimate=pl.CostEstimate(flops=2 * 10**9, bytes_accessed=12 * 2**20, transcendentals=0),
    )(in_smem(a_list), in_smem(b_list), in_vmem(b_clear), in_vmem(a_sorted), *(b for _, b in early))[:2]
    return pl.pallas_call(
        functools.partial(last_kernel, sz),
        out_shape=[
            pltpu.VMEM((LR * bs, width), jnp.float32),
            jax.ShapeDtypeStruct((LR * bs, width), jnp.float32),
        ],
        in_specs=[smem, vmem, pl.BlockSpec(memory_space=pl.ANY), vmem] + [vmem] * len(late),
        out_specs=[vmem, pl.BlockSpec(memory_space=pl.ANY)],
        input_output_aliases={1: 0, 2: 1},
        scratch_shapes=[
            pltpu.VMEM((len(sz.late), bs, bs), dtype),
            pltpu.VMEM((AT_ONCE, bs, bs), jnp.float32),
            pltpu.SemaphoreType.DMA,
        ],
        compiler_params=params,
    )(in_smem(late_list), in_vmem(total), out, in_vmem(a_sorted), *late)[1]


def solution(mesh):
    in_specs = (P("row", "col", None), P("row", "col"), P())
    out_specs = P("row", "col")
    return jax.shard_map(
        per_device, mesh=mesh, in_specs=in_specs, out_specs=out_specs, check_vma=False
    )
```

```python
import functools

import jax
import jax.numpy as jnp
from jax import lax
from jax.experimental import pallas as pl
from jax.experimental.pallas import tpu as pltpu
from jax.sharding import PartitionSpec as P

LR = 8
PW = 4
SECTIONS = 4
QD = 10
QS = 2
NOTE = 16
AT_ONCE = 8


class Sizes:
    def __init__(self, rows, cols, slots, bs):
        self.rows, self.cols, self.slots, self.bs = rows, cols, slots, bs
        self.lc = LR * rows // cols
        self.panels = rows * LR // PW
        panel_most = (self.lc // PW) * QS + (QD - QS)
        self.share = -(-panel_most // rows)
        self.near = -(-max(0, slots - rows * self.share) // self.share)
        self.held = SECTIONS * self.share
        self.depth = SECTIONS * PW
        self.late = [d * self.held + h for d in range(rows) if d & 1 and d & (rows // 2) for h in range(self.held)]

    def given(self, d):
        return self.share * (2 if d < self.near else 1)


def list_sections(sz, panels_ref, section_ref):
    for p in range(sz.panels):
        section_ref[p] = -1
    for j in range(SECTIONS):
        section_ref[panels_ref[j]] = j


def owned_by(panels_ref, row):
    count, first, last = jnp.int32(0), jnp.int32(-1), jnp.int32(0)
    for j in reversed(range(SECTIONS)):
        mine = lax.div(panels_ref[j], LR // PW) == row
        last = jnp.where(mine & (count == 0), j, last)
        first = jnp.where(mine, j, first)
        count = count + mine.astype(jnp.int32)
    return count, first, last


def deal(sz, count, picked, e, i):
    i = jnp.where(picked, i + 1, i)
    full = i == jnp.where((count == 2) & (e < sz.near), 2 * sz.share, sz.share)
    return jnp.where(full, e + 1, e), jnp.where(full, 0, i)


def pack_kernel(sz, pos_ref, panels_ref, pos_row_ref, x_ref, *refs):
    outs, (all_ref, section_ref, plan_ref, src_ref) = refs[: sz.rows], refs[sz.rows :]
    row = lax.axis_index("row")
    count, _, _ = owned_by(panels_ref, row)
    bs, most = sz.bs, 2 * sz.share
    for e in range(sz.rows * most):
        src_ref[e] = 0
    list_sections(sz, panels_ref, section_ref)
    for d in range(sz.rows):
        for i, value in enumerate(owned_by(panels_ref, row ^ d)):
            plan_ref[3 * d + i] = value

    e, i = jnp.int32(0), jnp.int32(0)
    for s in range(sz.slots):
        picked = section_ref[row * (LR // PW) + lax.div(pos_ref[0, s], sz.lc * PW)] >= 0

        @pl.when(picked)
        def _():
            src_ref[e * most + i] = s

        e, i = deal(sz, count, picked, e, i)
    note = jnp.broadcast_to(pos_row_ref[...].astype(jnp.float32), (NOTE, sz.slots)).astype(x_ref.dtype)
    for e in range(sz.rows):
        for i in range(sz.given(e)):
            outs[e][i * bs : (i + 1) * bs] = x_ref[src_ref[e * most + i]]
        outs[e][sz.given(e) * bs :, : sz.slots] = note
    for s in range(sz.slots):
        all_ref[s * bs : (s + 1) * bs] = x_ref[s]
    all_ref[sz.slots * bs :, : sz.slots] = note


def hold_kernel(sz, plan_ref, *refs):
    came, hold_ref, notes_ref = refs[: sz.rows], refs[sz.rows], refs[sz.rows + 1]
    n = sz.share * sz.bs

    for d in range(sz.rows):
        note = came[d][sz.given(d) * sz.bs :].astype(jnp.float32)[:1, : sz.slots]
        notes_ref[d : d + 1, :] = note.astype(jnp.int32)
    for d in range(sz.rows):
        count, first, last = (plan_ref[3 * d + i] for i in range(3))

        @pl.when(count > 0)
        def _():
            hold_ref[pl.ds(pl.multiple_of(first * n, n), n)] = came[d][:n]

        if d < sz.near:

            @pl.when(count == 2)
            def _():
                hold_ref[pl.ds(pl.multiple_of(last * n, n), n)] = came[d][n : 2 * n]


def column_meta_kernel(sz, notes_ref, section_ref, plan_ref, b_list, b_dense):
    row = lax.axis_index("row")
    b_dense[...] = jnp.zeros_like(b_dense)

    for i in range(sz.rows * sz.held):
        b_list[i] = -1

    def one_row(d, _):
        count, first, last = (plan_ref[3 * d + i] for i in range(3))
        owner = row ^ d

        def one(s, state):
            e, i = state
            pos = notes_ref[d, s]
            local_row, local_col = lax.div(pos, sz.lc), lax.rem(pos, sz.lc)
            section = section_ref[owner * (LR // PW) + lax.div(local_row, PW)]
            picked = section >= 0

            @pl.when(picked)
            def _():
                at = jnp.where(i < sz.share, first * sz.share + i, last * sz.share + i - sz.share)
                b_list[(d ^ e) * sz.held + at] = (section * PW + lax.rem(local_row, PW)) * sz.lc + local_col

            return deal(sz, count, picked, e, i)

        @pl.when(count > 0)
        def _():
            lax.fori_loop(0, sz.slots, one, (jnp.int32(0), jnp.int32(0)))

        return 0

    lax.fori_loop(0, sz.rows, one_row, 0)


def row_meta_kernel(sz, notes_ref, section_ref, b_list, *refs):
    a_refs, (a_list, late_list, a_sorted, by_k, latest) = refs[: sz.cols], refs[sz.cols :]
    col = lax.axis_index("col")
    bs, depth = sz.bs, sz.depth
    for i in range(LR):
        a_list[i * (depth + 1)] = 0
    for k in range(depth):
        by_k[k * (LR + 1)] = 0

    for e in range(sz.cols):

        def one(s, _):
            pos = notes_ref[e, s]
            local_row, local_col = lax.div(pos, sz.lc), lax.rem(pos, sz.lc)
            section = section_ref[(e ^ col) * (sz.lc // PW) + lax.div(local_col, PW)]

            @pl.when(section >= 0)
            def _():
                k = section * PW + lax.rem(local_col, PW)
                base = local_row * (depth + 1)
                n = a_list[base]
                a_list[base + 1 + n] = k
                a_list[base] = n + 1
                place = local_row * depth + n
                base = k * (LR + 1)
                n = by_k[base]
                by_k[base + 1 + n] = place
                by_k[base] = n + 1
                a_sorted[place] = a_refs[e][pl.ds(pl.multiple_of(s * bs, bs), bs), :]

            return 0

        lax.fori_loop(0, sz.slots, one, 0)

    total = jnp.int32(0)
    for h, at_place in enumerate(sz.late):
        at = b_list[at_place]
        there = at >= 0
        at = jnp.maximum(at, 0)
        base, c = lax.div(at, sz.lc) * (LR + 1), lax.rem(at, sz.lc)
        n = jnp.where(there, by_k[base], 0)

        def pair(t, _):
            place = by_k[base + 1 + t]
            tile = lax.div(place, depth) * sz.lc + c
            late_list[2 + 2 * (total + t)] = h * (LR * depth) + place
            late_list[3 + 2 * (total + t)] = tile
            latest[tile] = total + t
            return 0

        lax.fori_loop(0, n, pair, 0)
        total = total + n

    def mark(t, tiles):
        tile = late_list[3 + 2 * t]
        last = (latest[tile] == t).astype(jnp.int32)
        late_list[3 + 2 * t] = 2 * tile + last
        return tiles + last

    late_list[0] = total
    late_list[1] = lax.fori_loop(0, total, mark, jnp.int32(0))


def tile(sz, i, c):
    return pl.ds(pl.multiple_of(i * sz.bs, sz.bs), sz.bs), pl.ds(pl.multiple_of(c * sz.bs, sz.bs), sz.bs)


def product_kernel(sz, starts, a_list, b_list, b_clear, a_sorted, *refs):
    b_refs, (total, out_ref, b_dense, sem) = refs[: len(starts)], refs[len(starts) :]
    bs, depth = sz.bs, sz.depth
    for start, b_ref in zip(starts, b_refs):
        for h in range(b_ref.shape[0] // bs):
            at = b_list[start + h]

            @pl.when(at >= 0)
            def _():
                k, c = lax.div(at, sz.lc), lax.rem(at, sz.lc)
                b_dense[k, :, pl.ds(pl.multiple_of(c * bs, bs), bs)] = b_ref[h * bs : (h + 1) * bs]

    width = total.shape[1]
    chunk = min(width, 512)

    def to_out(i):
        here = pl.ds(pl.multiple_of(i * bs, bs), bs)
        return pltpu.make_async_copy(total.at[here], out_ref.at[here], sem)

    def one_row(i, _):
        base = i * (depth + 1)
        n = a_list[base]
        here = pl.ds(pl.multiple_of(i * bs, bs), bs)

        def group(start, size, first):
            ks, blocks = [], []
            for t in range(size):
                at = jnp.minimum(start + t, depth - 1)
                there = start + t < n
                block = a_sorted[i * depth + at]
                blocks.append(jnp.where(there, block, jnp.zeros_like(block)))
                ks.append(jnp.where(there, a_list[base + 1 + at], 0))
            lhs = jnp.concatenate(blocks, axis=1)
            for c in range(0, width, chunk):
                rhs = jnp.concatenate([b_dense[k, :, c : c + chunk] for k in ks], axis=0)
                part = jnp.dot(lhs, rhs, preferred_element_type=jnp.float32)
                if first:
                    total[here, c : c + chunk] = part
                else:
                    total[here, c : c + chunk] += part

        @pl.when(n <= 2)
        def _():
            group(0, 2, True)

        @pl.when(n > 2)
        def _():
            group(0, 4, True)

        def more(g, _):
            group(4 + 2 * g, 2, False)
            return 0

        lax.fori_loop(0, lax.div(jnp.maximum(n - 3, 0), 2), more, 0)
        to_out(i).start()
        return 0

    lax.fori_loop(0, LR, one_row, 0)

    def done(i, _):
        to_out(i).wait()
        return 0

    lax.fori_loop(0, LR, done, 0)


def last_kernel(sz, late_list, total_in, out_in, a_sorted, *refs):
    b_refs, (total, out_ref, right, sem) = refs[:-4], refs[-4:]
    bs, every = sz.bs, LR * sz.depth
    count = late_list[0]
    at = 0
    for b_ref in b_refs:
        for h in range(b_ref.shape[0] // bs):
            right[at] = b_ref[h * bs : (h + 1) * bs]
            at += 1

    def to_out(at):
        return pltpu.make_async_copy(total.at[at], out_ref.at[at], sem)

    def place(t):
        code = late_list[3 + 2 * t]
        return tile(sz, lax.div(code, 2 * sz.lc), lax.rem(lax.div(code, 2), sz.lc)), lax.rem(code, 2) == 1

    def group(g, _):
        for u in range(AT_ONCE):
            t = g * AT_ONCE + u
            at = jnp.minimum(t, count - 1)
            code = late_list[2 + 2 * at]
            part = jnp.dot(
                a_sorted[lax.rem(code, every)], right[lax.div(code, every)], preferred_element_type=jnp.float32
            )
            total[place(at)[0]] += jnp.where(t < count, part, 0.0)
        for u in range(AT_ONCE):
            t = g * AT_ONCE + u
            at, last = place(jnp.minimum(t, count - 1))

            @pl.when((t < count) & last)
            def _():
                to_out(at).start()

        return 0

    lax.fori_loop(0, lax.div(count + AT_ONCE - 1, AT_ONCE), group, 0)

    def done(t, _):
        to_out((slice(0, bs), slice(0, bs))).wait()
        return 0

    lax.fori_loop(0, late_list[1], done, 0)


def flip(x, axis, d):
    return lax.ppermute(x, axis, [(i, i ^ d) for i in range(lax.axis_size(axis))])


def gather_by_flips(x, axis):
    n = lax.axis_size(axis)
    got, bit = {0: x}, n // 2
    while bit:
        for d in list(got):
            got[d | bit] = flip(got[d], axis, bit)
        bit //= 2
    return [got[d] for d in range(n)]


def per_device(x_tiles, tile_pos, panel_ids):
    rows, cols = lax.axis_size("row"), lax.axis_size("col")
    slots, bs, _ = x_tiles.shape
    dtype = x_tiles.dtype
    sz = Sizes(rows, cols, slots, bs)
    smem = pl.BlockSpec(memory_space=pltpu.SMEM)
    vmem = pl.BlockSpec(memory_space=pltpu.VMEM)

    *parts, mine, sections, plan = pl.pallas_call(
        functools.partial(pack_kernel, sz),
        out_shape=[pltpu.VMEM((sz.given(d) * bs + NOTE, bs), dtype) for d in range(rows)]
        + [
            pltpu.VMEM((slots * bs + NOTE, bs), dtype),
            pltpu.SMEM((sz.panels,), jnp.int32),
            pltpu.SMEM((3 * rows,), jnp.int32),
        ],
        in_specs=[smem, smem, vmem, vmem],
        out_specs=[vmem] * (rows + 1) + [smem, smem],
        scratch_shapes=[pltpu.SMEM((rows * 2 * sz.share,), jnp.int32)],
    )(tile_pos, panel_ids, tile_pos, x_tiles)

    in_vmem = functools.partial(pltpu.with_memory_space_constraint, memory_space=pltpu.VMEM)
    in_smem = functools.partial(pltpu.with_memory_space_constraint, memory_space=pltpu.SMEM)
    sections, plan = in_smem(sections), in_smem(plan)
    a_got, a_bit = {0: mine}, cols // 2
    a_got[a_bit] = flip(mine, "col", a_bit)
    came = [parts[0]] + [flip(parts[d], "row", d) for d in range(1, rows)]
    hold, column_notes = pl.pallas_call(
        functools.partial(hold_kernel, sz),
        out_shape=[
            pltpu.VMEM((sz.held * bs, bs), dtype),
            jax.ShapeDtypeStruct((rows, slots), jnp.int32),
        ],
        in_specs=[smem] + [vmem] * rows,
        out_specs=[vmem, vmem],
    )(plan, *map(in_vmem, came))
    width = sz.lc * bs
    params = pltpu.CompilerParams(vmem_limit_bytes=32 * 2**20)
    b_list, b_clear = pl.pallas_call(
        functools.partial(column_meta_kernel, sz),
        out_shape=[
            pltpu.SMEM((rows * sz.held,), jnp.int32),
            pltpu.VMEM((sz.depth, bs, width), dtype),
        ],
        in_specs=[smem, smem, smem],
        out_specs=[smem, vmem],
        compiler_params=params,
    )(column_notes, sections, plan)

    bits = [1 << b for b in reversed(range(rows.bit_length() - 1))]
    a_got, hold_too = lax.optimization_barrier((a_got, hold))
    got = {0: [hold], **{bit: [flip(hold_too if bit < bits[0] else hold, "row", bit)] for bit in bits}}
    while a_bit:
        for d in list(a_got):
            if d | a_bit not in a_got:
                a_got[d | a_bit] = flip(a_got[d], "col", a_bit)
        a_bit //= 2
    a_parts = [a_got[d] for d in range(cols)]
    row_notes = jnp.stack([a[-1, :slots] for a in a_parts]).astype(jnp.int32)
    a_list, late_list, a_sorted = pl.pallas_call(
        functools.partial(row_meta_kernel, sz),
        out_shape=[
            pltpu.SMEM((LR * (sz.depth + 1),), jnp.int32),
            pltpu.SMEM((2 + 2 * len(sz.late) * LR,), jnp.int32),
            pltpu.VMEM((LR * sz.depth, bs, bs), dtype),
        ],
        in_specs=[smem] * 3 + [vmem] * cols,
        out_specs=[smem, smem, vmem],
        scratch_shapes=[
            pltpu.SMEM((sz.depth * (LR + 1),), jnp.int32),
            pltpu.SMEM((LR * sz.lc,), jnp.int32),
        ],
        compiler_params=params,
    )(row_notes, sections, in_smem(b_list), *map(in_vmem, a_parts))
    got[2], a_list, a_sorted = lax.optimization_barrier((got[2], a_list, a_sorted))
    if 3 not in got:
        got[3] = [flip(got[2][0], "row", 1)]
    (top, second), half = bits[:2], sz.held * bs // 2
    got[top], got[2], got[1], a_list, a_sorted = lax.optimization_barrier(
        (got[top], got[2], got[1], a_list, a_sorted)
    )
    first, rest = got[top][0][:half], got[top][0][half:]
    first, rest = flip(first, "row", second), flip(rest, "row", second)
    got[top | second] = [first, rest]
    got[top | second | 1] = [flip(p, "row", 1) for p in got[top | second]]
    got[top | 1] = [flip(got[top][0][:half], "row", 1), flip(got[1][0][half:], "row", top)]
    for bit in bits[1:]:
        for d in list(got):
            if d | bit not in got:
                got[d | bit] = [flip(p, "row", bit) for p in got[d]]

    early, late = [], []
    for d in range(rows):
        for i, piece in enumerate(got[d]):
            if d * sz.held in sz.late:
                late.append(in_vmem(piece))
            else:
                early.append((d * sz.held + i * half // bs, in_vmem(piece)))

    total, out = pl.pallas_call(
        functools.partial(product_kernel, sz, [start for start, _ in early]),
        out_shape=[
            pltpu.VMEM((LR * bs, width), jnp.float32),
            jax.ShapeDtypeStruct((LR * bs, width), jnp.float32),
            pltpu.VMEM((sz.depth, bs, width), dtype),
        ],
        in_specs=[smem, smem] + [vmem] * (2 + len(early)),
        out_specs=[vmem, pl.BlockSpec(memory_space=pl.ANY), vmem],
        input_output_aliases={2: 2},
        scratch_shapes=[pltpu.SemaphoreType.DMA],
        compiler_params=params,
        cost_estimate=pl.CostEstimate(flops=2 * 10**9, bytes_accessed=12 * 2**20, transcendentals=0),
    )(in_smem(a_list), in_smem(b_list), in_vmem(b_clear), in_vmem(a_sorted), *(b for _, b in early))[:2]
    return pl.pallas_call(
        functools.partial(last_kernel, sz),
        out_shape=[
            pltpu.VMEM((LR * bs, width), jnp.float32),
            jax.ShapeDtypeStruct((LR * bs, width), jnp.float32),
        ],
        in_specs=[smem, vmem, pl.BlockSpec(memory_space=pl.ANY), vmem] + [vmem] * len(late),
        out_specs=[vmem, pl.BlockSpec(memory_space=pl.ANY)],
        input_output_aliases={1: 0, 2: 1},
        scratch_shapes=[
            pltpu.VMEM((len(sz.late), bs, bs), dtype),
            pltpu.SemaphoreType.DMA,
        ],
        compiler_params=params,
    )(in_smem(late_list), in_vmem(total), out, in_vmem(a_sorted), *late)[1]


def solution(mesh):
    in_specs = (P("row", "col", None), P("row", "col"), P())
    out_specs = P("row", "col")
    return jax.shard_map(
        per_device, mesh=mesh, in_specs=in_specs, out_specs=out_specs, check_vma=False
    )
```

```python
import functools

import jax
import jax.numpy as jnp
from jax import lax
from jax.experimental import pallas as pl
from jax.experimental.pallas import tpu as pltpu
from jax.sharding import PartitionSpec as P

LR = 8
PW = 4
SECTIONS = 4
QD = 10
QS = 2
NOTE = 16
AT_ONCE = 8


class Sizes:
    def __init__(self, rows, cols, slots, bs):
        self.rows, self.cols, self.slots, self.bs = rows, cols, slots, bs
        self.lc = LR * rows // cols
        self.panels = rows * LR // PW
        panel_most = (self.lc // PW) * QS + (QD - QS)
        self.share = -(-panel_most // rows)
        self.near = -(-max(0, slots - rows * self.share) // self.share)
        self.held = SECTIONS * self.share
        self.depth = SECTIONS * PW
        self.late = [d * self.held + h for d in range(rows) if d & 1 and d & (rows // 2) for h in range(self.held)]

    def given(self, d):
        return self.share * (2 if d < self.near else 1)


def list_sections(sz, panels_ref, section_ref):
    for p in range(sz.panels):
        section_ref[p] = -1
    for j in range(SECTIONS):
        section_ref[panels_ref[j]] = j


def owned_by(panels_ref, row):
    count, first, last = jnp.int32(0), jnp.int32(-1), jnp.int32(0)
    for j in reversed(range(SECTIONS)):
        mine = lax.div(panels_ref[j], LR // PW) == row
        last = jnp.where(mine & (count == 0), j, last)
        first = jnp.where(mine, j, first)
        count = count + mine.astype(jnp.int32)
    return count, first, last


def deal(sz, count, picked, e, i):
    i = jnp.where(picked, i + 1, i)
    full = i == jnp.where((count == 2) & (e < sz.near), 2 * sz.share, sz.share)
    return jnp.where(full, e + 1, e), jnp.where(full, 0, i)


def pack_kernel(sz, pos_ref, panels_ref, pos_row_ref, x_ref, *refs):
    outs, (all_ref, section_ref, plan_ref, src_ref) = refs[: sz.rows], refs[sz.rows :]
    row = lax.axis_index("row")
    count, _, _ = owned_by(panels_ref, row)
    bs, most = sz.bs, 2 * sz.share
    for e in range(sz.rows * most):
        src_ref[e] = 0
    list_sections(sz, panels_ref, section_ref)
    for d in range(sz.rows):
        for i, value in enumerate(owned_by(panels_ref, row ^ d)):
            plan_ref[3 * d + i] = value

    e, i = jnp.int32(0), jnp.int32(0)
    for s in range(sz.slots):
        picked = section_ref[row * (LR // PW) + lax.div(pos_ref[0, s], sz.lc * PW)] >= 0

        @pl.when(picked)
        def _():
            src_ref[e * most + i] = s

        e, i = deal(sz, count, picked, e, i)
    note = jnp.broadcast_to(pos_row_ref[...].astype(jnp.float32), (NOTE, sz.slots)).astype(x_ref.dtype)
    for e in range(sz.rows):
        for i in range(sz.given(e)):
            outs[e][i * bs : (i + 1) * bs] = x_ref[src_ref[e * most + i]]
        outs[e][sz.given(e) * bs :, : sz.slots] = note
    for s in range(sz.slots):
        all_ref[s * bs : (s + 1) * bs] = x_ref[s]
    all_ref[sz.slots * bs :, : sz.slots] = note


def hold_kernel(sz, plan_ref, *refs):
    came, hold_ref, notes_ref = refs[: sz.rows], refs[sz.rows], refs[sz.rows + 1]
    n = sz.share * sz.bs

    for d in range(sz.rows):
        note = came[d][sz.given(d) * sz.bs :].astype(jnp.float32)[:1, : sz.slots]
        notes_ref[d : d + 1, :] = note.astype(jnp.int32)
    for d in range(sz.rows):
        count, first, last = (plan_ref[3 * d + i] for i in range(3))

        @pl.when(count > 0)
        def _():
            hold_ref[pl.ds(pl.multiple_of(first * n, n), n)] = came[d][:n]

        if d < sz.near:

            @pl.when(count == 2)
            def _():
                hold_ref[pl.ds(pl.multiple_of(last * n, n), n)] = came[d][n : 2 * n]


def column_meta_kernel(sz, notes_ref, section_ref, plan_ref, b_list, b_dense):
    row = lax.axis_index("row")
    b_dense[...] = jnp.zeros_like(b_dense)

    for i in range(sz.rows * sz.held):
        b_list[i] = -1

    def one_row(d, _):
        count, first, last = (plan_ref[3 * d + i] for i in range(3))
        owner = row ^ d

        def one(s, state):
            e, i = state
            pos = notes_ref[d, s]
            local_row, local_col = lax.div(pos, sz.lc), lax.rem(pos, sz.lc)
            section = section_ref[owner * (LR // PW) + lax.div(local_row, PW)]
            picked = section >= 0

            @pl.when(picked)
            def _():
                at = jnp.where(i < sz.share, first * sz.share + i, last * sz.share + i - sz.share)
                b_list[(d ^ e) * sz.held + at] = (section * PW + lax.rem(local_row, PW)) * sz.lc + local_col

            return deal(sz, count, picked, e, i)

        @pl.when(count > 0)
        def _():
            lax.fori_loop(0, sz.slots, one, (jnp.int32(0), jnp.int32(0)))

        return 0

    lax.fori_loop(0, sz.rows, one_row, 0)


def row_meta_kernel(sz, notes_ref, section_ref, b_list, *refs):
    a_refs, (a_list, late_list, a_sorted, by_k, latest) = refs[: sz.cols], refs[sz.cols :]
    col = lax.axis_index("col")
    bs, depth = sz.bs, sz.depth
    for i in range(LR):
        a_list[i * (depth + 1)] = 0
    for k in range(depth):
        by_k[k * (LR + 1)] = 0

    for e in range(sz.cols):

        def one(s, _):
            pos = notes_ref[e, s]
            local_row, local_col = lax.div(pos, sz.lc), lax.rem(pos, sz.lc)
            section = section_ref[(e ^ col) * (sz.lc // PW) + lax.div(local_col, PW)]

            @pl.when(section >= 0)
            def _():
                k = section * PW + lax.rem(local_col, PW)
                base = local_row * (depth + 1)
                n = a_list[base]
                a_list[base + 1 + n] = k
                a_list[base] = n + 1
                place = local_row * depth + n
                base = k * (LR + 1)
                n = by_k[base]
                by_k[base + 1 + n] = place
                by_k[base] = n + 1
                a_sorted[place] = a_refs[e][pl.ds(pl.multiple_of(s * bs, bs), bs), :]

            return 0

        lax.fori_loop(0, sz.slots, one, 0)

    total = jnp.int32(0)
    for h, at_place in enumerate(sz.late):
        at = b_list[at_place]
        there = at >= 0
        at = jnp.maximum(at, 0)
        base, c = lax.div(at, sz.lc) * (LR + 1), lax.rem(at, sz.lc)
        n = jnp.where(there, by_k[base], 0)

        def pair(t, _):
            place = by_k[base + 1 + t]
            tile = lax.div(place, depth) * sz.lc + c
            late_list[2 + 2 * (total + t)] = h * (LR * depth) + place
            late_list[3 + 2 * (total + t)] = tile
            latest[tile] = total + t
            return 0

        lax.fori_loop(0, n, pair, 0)
        total = total + n

    def mark(t, tiles):
        tile = late_list[3 + 2 * t]
        last = (latest[tile] == t).astype(jnp.int32)
        late_list[3 + 2 * t] = 2 * tile + last
        return tiles + last

    late_list[0] = total
    late_list[1] = lax.fori_loop(0, total, mark, jnp.int32(0))


def tile(sz, i, c):
    return pl.ds(pl.multiple_of(i * sz.bs, sz.bs), sz.bs), pl.ds(pl.multiple_of(c * sz.bs, sz.bs), sz.bs)


def product_kernel(sz, starts, a_list, b_list, b_clear, a_sorted, *refs):
    b_refs, (total, out_ref, b_dense, sem) = refs[: len(starts)], refs[len(starts) :]
    bs, depth = sz.bs, sz.depth
    for start, b_ref in zip(starts, b_refs):
        for h in range(b_ref.shape[0] // bs):
            at = b_list[start + h]

            @pl.when(at >= 0)
            def _():
                k, c = lax.div(at, sz.lc), lax.rem(at, sz.lc)
                b_dense[k, :, pl.ds(pl.multiple_of(c * bs, bs), bs)] = b_ref[h * bs : (h + 1) * bs]

    width = total.shape[1]
    chunk = min(width, 512)

    def to_out(i):
        here = pl.ds(pl.multiple_of(i * bs, bs), bs)
        return pltpu.make_async_copy(total.at[here], out_ref.at[here], sem)

    def one_row(i, _):
        base = i * (depth + 1)
        n = a_list[base]
        here = pl.ds(pl.multiple_of(i * bs, bs), bs)

        def group(start, size, first):
            ks, blocks = [], []
            for t in range(size):
                at = jnp.minimum(start + t, depth - 1)
                there = start + t < n
                block = a_sorted[i * depth + at]
                blocks.append(jnp.where(there, block, jnp.zeros_like(block)))
                ks.append(jnp.where(there, a_list[base + 1 + at], 0))
            lhs = jnp.concatenate(blocks, axis=1)
            for c in range(0, width, chunk):
                rhs = jnp.concatenate([b_dense[k, :, c : c + chunk] for k in ks], axis=0)
                part = jnp.dot(lhs, rhs, preferred_element_type=jnp.float32)
                if first:
                    total[here, c : c + chunk] = part
                else:
                    total[here, c : c + chunk] += part

        @pl.when(n <= 2)
        def _():
            group(0, 2, True)

        @pl.when(n > 2)
        def _():
            group(0, 4, True)

        def more(g, _):
            group(4 + 2 * g, 2, False)
            return 0

        lax.fori_loop(0, lax.div(jnp.maximum(n - 3, 0), 2), more, 0)
        to_out(i).start()
        return 0

    lax.fori_loop(0, LR, one_row, 0)

    def done(i, _):
        to_out(i).wait()
        return 0

    lax.fori_loop(0, LR, done, 0)


def last_kernel(sz, late_list, total_in, out_in, a_sorted, *refs):
    b_refs, (total, out_ref, right, sem) = refs[:-4], refs[-4:]
    bs, every = sz.bs, LR * sz.depth
    count = late_list[0]
    at = 0
    for b_ref in b_refs:
        for h in range(b_ref.shape[0] // bs):
            right[at] = b_ref[h * bs : (h + 1) * bs]
            at += 1

    def to_out(at):
        return pltpu.make_async_copy(total.at[at], out_ref.at[at], sem)

    def place(t):
        code = late_list[3 + 2 * t]
        return tile(sz, lax.div(code, 2 * sz.lc), lax.rem(lax.div(code, 2), sz.lc)), lax.rem(code, 2) == 1

    def group(g, _):
        for u in range(AT_ONCE):
            t = g * AT_ONCE + u
            at = jnp.minimum(t, count - 1)
            code = late_list[2 + 2 * at]
            part = jnp.dot(
                a_sorted[lax.rem(code, every)], right[lax.div(code, every)], preferred_element_type=jnp.float32
            )
            total[place(at)[0]] += jnp.where(t < count, part, 0.0)
        for u in range(AT_ONCE):
            t = g * AT_ONCE + u
            at, last = place(jnp.minimum(t, count - 1))

            @pl.when((t < count) & last)
            def _():
                to_out(at).start()

        return 0

    lax.fori_loop(0, lax.div(count + AT_ONCE - 1, AT_ONCE), group, 0)

    def done(t, _):
        to_out((slice(0, bs), slice(0, bs))).wait()
        return 0

    lax.fori_loop(0, late_list[1], done, 0)


def flip(x, axis, d):
    return lax.ppermute(x, axis, [(i, i ^ d) for i in range(lax.axis_size(axis))])


def gather_by_flips(x, axis):
    n = lax.axis_size(axis)
    got, bit = {0: x}, n // 2
    while bit:
        for d in list(got):
            got[d | bit] = flip(got[d], axis, bit)
        bit //= 2
    return [got[d] for d in range(n)]


def per_device(x_tiles, tile_pos, panel_ids):
    rows, cols = lax.axis_size("row"), lax.axis_size("col")
    slots, bs, _ = x_tiles.shape
    dtype = x_tiles.dtype
    sz = Sizes(rows, cols, slots, bs)
    smem = pl.BlockSpec(memory_space=pltpu.SMEM)
    vmem = pl.BlockSpec(memory_space=pltpu.VMEM)

    *parts, mine, sections, plan = pl.pallas_call(
        functools.partial(pack_kernel, sz),
        out_shape=[pltpu.VMEM((sz.given(d) * bs + NOTE, bs), dtype) for d in range(rows)]
        + [
            pltpu.VMEM((slots * bs + NOTE, bs), dtype),
            pltpu.SMEM((sz.panels,), jnp.int32),
            pltpu.SMEM((3 * rows,), jnp.int32),
        ],
        in_specs=[smem, smem, vmem, vmem],
        out_specs=[vmem] * (rows + 1) + [smem, smem],
        scratch_shapes=[pltpu.SMEM((rows * 2 * sz.share,), jnp.int32)],
    )(tile_pos, panel_ids, tile_pos, x_tiles)

    in_vmem = functools.partial(pltpu.with_memory_space_constraint, memory_space=pltpu.VMEM)
    in_smem = functools.partial(pltpu.with_memory_space_constraint, memory_space=pltpu.SMEM)
    sections, plan = in_smem(sections), in_smem(plan)
    a_got, a_bit = {0: mine}, cols // 2
    a_got[a_bit] = flip(mine, "col", a_bit)
    came = [parts[0]]
    for d in range(1, rows):
        if d == rows - 2:
            parts[d], came[1] = lax.optimization_barrier((parts[d], came[1]))
        came.append(flip(parts[d], "row", d))
    hold, column_notes = pl.pallas_call(
        functools.partial(hold_kernel, sz),
        out_shape=[
            pltpu.VMEM((sz.held * bs, bs), dtype),
            jax.ShapeDtypeStruct((rows, slots), jnp.int32),
        ],
        in_specs=[smem] + [vmem] * rows,
        out_specs=[vmem, vmem],
    )(plan, *map(in_vmem, came))
    width = sz.lc * bs
    params = pltpu.CompilerParams(vmem_limit_bytes=32 * 2**20)
    b_list, b_clear = pl.pallas_call(
        functools.partial(column_meta_kernel, sz),
        out_shape=[
            pltpu.SMEM((rows * sz.held,), jnp.int32),
            pltpu.VMEM((sz.depth, bs, width), dtype),
        ],
        in_specs=[smem, smem, smem],
        out_specs=[smem, vmem],
        compiler_params=params,
    )(column_notes, sections, plan)

    bits = [1 << b for b in reversed(range(rows.bit_length() - 1))]
    a_got, hold_too = lax.optimization_barrier((a_got, hold))
    got = {0: [hold], **{bit: [flip(hold_too if bit < bits[0] else hold, "row", bit)] for bit in bits}}
    while a_bit:
        for d in list(a_got):
            if d | a_bit not in a_got:
                a_got[d | a_bit] = flip(a_got[d], "col", a_bit)
        a_bit //= 2
    a_parts = [a_got[d] for d in range(cols)]
    row_notes = jnp.stack([a[-1, :slots] for a in a_parts]).astype(jnp.int32)
    a_list, late_list, a_sorted = pl.pallas_call(
        functools.partial(row_meta_kernel, sz),
        out_shape=[
            pltpu.SMEM((LR * (sz.depth + 1),), jnp.int32),
            pltpu.SMEM((2 + 2 * len(sz.late) * LR,), jnp.int32),
            pltpu.VMEM((LR * sz.depth, bs, bs), dtype),
        ],
        in_specs=[smem] * 3 + [vmem] * cols,
        out_specs=[smem, smem, vmem],
        scratch_shapes=[
            pltpu.SMEM((sz.depth * (LR + 1),), jnp.int32),
            pltpu.SMEM((LR * sz.lc,), jnp.int32),
        ],
        compiler_params=params,
    )(row_notes, sections, in_smem(b_list), *map(in_vmem, a_parts))
    got[2], a_list, a_sorted = lax.optimization_barrier((got[2], a_list, a_sorted))
    if 3 not in got:
        got[3] = [flip(got[2][0], "row", 1)]
    (top, second), half = bits[:2], sz.held * bs // 2
    got[top], got[2], got[1], a_list, a_sorted = lax.optimization_barrier(
        (got[top], got[2], got[1], a_list, a_sorted)
    )
    first, rest = got[top][0][:half], got[top][0][half:]
    first, rest = flip(first, "row", second), flip(rest, "row", second)
    got[top | second] = [first, rest]
    got[top | second | 1] = [flip(p, "row", 1) for p in got[top | second]]
    got[top | 1] = [flip(got[top][0][:half], "row", 1), flip(got[1][0][half:], "row", top)]
    for bit in bits[1:]:
        for d in list(got):
            if d | bit not in got:
                got[d | bit] = [flip(p, "row", bit) for p in got[d]]

    early, late = [], []
    for d in range(rows):
        for i, piece in enumerate(got[d]):
            if d * sz.held in sz.late:
                late.append(in_vmem(piece))
            else:
                early.append((d * sz.held + i * half // bs, in_vmem(piece)))

    total, out = pl.pallas_call(
        functools.partial(product_kernel, sz, [start for start, _ in early]),
        out_shape=[
            pltpu.VMEM((LR * bs, width), jnp.float32),
            jax.ShapeDtypeStruct((LR * bs, width), jnp.float32),
            pltpu.VMEM((sz.depth, bs, width), dtype),
        ],
        in_specs=[smem, smem] + [vmem] * (2 + len(early)),
        out_specs=[vmem, pl.BlockSpec(memory_space=pl.ANY), vmem],
        input_output_aliases={2: 2},
        scratch_shapes=[pltpu.SemaphoreType.DMA],
        compiler_params=params,
        cost_estimate=pl.CostEstimate(flops=2 * 10**9, bytes_accessed=12 * 2**20, transcendentals=0),
    )(in_smem(a_list), in_smem(b_list), in_vmem(b_clear), in_vmem(a_sorted), *(b for _, b in early))[:2]
    return pl.pallas_call(
        functools.partial(last_kernel, sz),
        out_shape=[
            pltpu.VMEM((LR * bs, width), jnp.float32),
            jax.ShapeDtypeStruct((LR * bs, width), jnp.float32),
        ],
        in_specs=[smem, vmem, pl.BlockSpec(memory_space=pl.ANY), vmem] + [vmem] * len(late),
        out_specs=[vmem, pl.BlockSpec(memory_space=pl.ANY)],
        input_output_aliases={1: 0, 2: 1},
        scratch_shapes=[
            pltpu.VMEM((len(sz.late), bs, bs), dtype),
            pltpu.SemaphoreType.DMA,
        ],
        compiler_params=params,
    )(in_smem(late_list), in_vmem(total), out, in_vmem(a_sorted), *late)[1]


def solution(mesh):
    in_specs = (P("row", "col", None), P("row", "col"), P())
    out_specs = P("row", "col")
    return jax.shard_map(
        per_device, mesh=mesh, in_specs=in_specs, out_specs=out_specs, check_vma=False
    )
```

```python
import functools

import jax
import jax.numpy as jnp
from jax import lax
from jax.experimental import pallas as pl
from jax.experimental.pallas import tpu as pltpu
from jax.sharding import PartitionSpec as P

LR = 8
PW = 4
SECTIONS = 4
QD = 10
QS = 2
NOTE = 16
AT_ONCE = 8


class Sizes:
    def __init__(self, rows, cols, slots, bs):
        self.rows, self.cols, self.slots, self.bs = rows, cols, slots, bs
        self.lc = LR * rows // cols
        self.panels = rows * LR // PW
        panel_most = (self.lc // PW) * QS + (QD - QS)
        self.share = -(-panel_most // rows)
        self.near = -(-max(0, slots - rows * self.share) // self.share)
        self.held = SECTIONS * self.share
        self.depth = SECTIONS * PW
        self.late = [d * self.held + h for d in range(rows) if d & 1 and d & (rows // 2) for h in range(self.held)]

    def given(self, d):
        return self.share * (2 if d < self.near else 1)


def list_sections(sz, panels_ref, section_ref):
    for p in range(sz.panels):
        section_ref[p] = -1
    for j in range(SECTIONS):
        section_ref[panels_ref[j]] = j


def owned_by(panels_ref, row):
    count, first, last = jnp.int32(0), jnp.int32(-1), jnp.int32(0)
    for j in reversed(range(SECTIONS)):
        mine = lax.div(panels_ref[j], LR // PW) == row
        last = jnp.where(mine & (count == 0), j, last)
        first = jnp.where(mine, j, first)
        count = count + mine.astype(jnp.int32)
    return count, first, last


def deal(sz, count, picked, e, i):
    i = jnp.where(picked, i + 1, i)
    full = i == jnp.where((count == 2) & (e < sz.near), 2 * sz.share, sz.share)
    return jnp.where(full, e + 1, e), jnp.where(full, 0, i)


def pack_kernel(sz, pos_ref, panels_ref, pos_row_ref, x_ref, *refs):
    outs, (all_ref, section_ref, plan_ref, src_ref) = refs[: sz.rows], refs[sz.rows :]
    row = lax.axis_index("row")
    count, _, _ = owned_by(panels_ref, row)
    bs, most = sz.bs, 2 * sz.share
    for e in range(sz.rows * most):
        src_ref[e] = 0
    list_sections(sz, panels_ref, section_ref)
    for d in range(sz.rows):
        for i, value in enumerate(owned_by(panels_ref, row ^ d)):
            plan_ref[3 * d + i] = value

    e, i = jnp.int32(0), jnp.int32(0)
    for s in range(sz.slots):
        picked = section_ref[row * (LR // PW) + lax.div(pos_ref[0, s], sz.lc * PW)] >= 0

        @pl.when(picked)
        def _():
            src_ref[e * most + i] = s

        e, i = deal(sz, count, picked, e, i)
    note = jnp.broadcast_to(pos_row_ref[...].astype(jnp.float32), (NOTE, sz.slots)).astype(x_ref.dtype)
    for e in range(sz.rows):
        for i in range(sz.given(e)):
            outs[e][i * bs : (i + 1) * bs] = x_ref[src_ref[e * most + i]]
        outs[e][sz.given(e) * bs :, : sz.slots] = note
    for s in range(sz.slots):
        all_ref[s * bs : (s + 1) * bs] = x_ref[s]
    all_ref[sz.slots * bs :, : sz.slots] = note


def hold_kernel(sz, plan_ref, *refs):
    came, hold_ref, notes_ref = refs[: sz.rows], refs[sz.rows], refs[sz.rows + 1]
    n = sz.share * sz.bs

    for d in range(sz.rows):
        note = came[d][sz.given(d) * sz.bs :].astype(jnp.float32)[:1, : sz.slots]
        notes_ref[d : d + 1, :] = note.astype(jnp.int32)
    for d in range(sz.rows):
        count, first, last = (plan_ref[3 * d + i] for i in range(3))

        @pl.when(count > 0)
        def _():
            hold_ref[pl.ds(pl.multiple_of(first * n, n), n)] = came[d][:n]

        if d < sz.near:

            @pl.when(count == 2)
            def _():
                hold_ref[pl.ds(pl.multiple_of(last * n, n), n)] = came[d][n : 2 * n]


def column_meta_kernel(sz, notes_ref, section_ref, plan_ref, b_list, b_dense):
    row = lax.axis_index("row")
    b_dense[...] = jnp.zeros_like(b_dense)

    for i in range(sz.rows * sz.held):
        b_list[i] = -1

    def one_row(d, _):
        count, first, last = (plan_ref[3 * d + i] for i in range(3))
        owner = row ^ d

        def one(s, state):
            e, i = state
            pos = notes_ref[d, s]
            local_row, local_col = lax.div(pos, sz.lc), lax.rem(pos, sz.lc)
            section = section_ref[owner * (LR // PW) + lax.div(local_row, PW)]
            picked = section >= 0

            @pl.when(picked)
            def _():
                at = jnp.where(i < sz.share, first * sz.share + i, last * sz.share + i - sz.share)
                b_list[(d ^ e) * sz.held + at] = (section * PW + lax.rem(local_row, PW)) * sz.lc + local_col

            return deal(sz, count, picked, e, i)

        @pl.when(count > 0)
        def _():
            lax.fori_loop(0, sz.slots, one, (jnp.int32(0), jnp.int32(0)))

        return 0

    lax.fori_loop(0, sz.rows, one_row, 0)


def row_meta_kernel(sz, notes_ref, section_ref, b_list, *refs):
    a_refs, (a_list, late_list, a_sorted, by_k, latest) = refs[: sz.cols], refs[sz.cols :]
    col = lax.axis_index("col")
    bs, depth = sz.bs, sz.depth
    for i in range(LR):
        a_list[i * (depth + 1)] = 0
    for k in range(depth):
        by_k[k * (LR + 1)] = 0

    for e in range(sz.cols):

        def one(s, _):
            pos = notes_ref[e, s]
            local_row, local_col = lax.div(pos, sz.lc), lax.rem(pos, sz.lc)
            section = section_ref[(e ^ col) * (sz.lc // PW) + lax.div(local_col, PW)]

            @pl.when(section >= 0)
            def _():
                k = section * PW + lax.rem(local_col, PW)
                base = local_row * (depth + 1)
                n = a_list[base]
                a_list[base + 1 + n] = k
                a_list[base] = n + 1
                place = local_row * depth + n
                base = k * (LR + 1)
                n = by_k[base]
                by_k[base + 1 + n] = place
                by_k[base] = n + 1
                a_sorted[place] = a_refs[e][pl.ds(pl.multiple_of(s * bs, bs), bs), :]

            return 0

        lax.fori_loop(0, sz.slots, one, 0)

    total = jnp.int32(0)
    for h, at_place in enumerate(sz.late):
        at = b_list[at_place]
        there = at >= 0
        at = jnp.maximum(at, 0)
        base, c = lax.div(at, sz.lc) * (LR + 1), lax.rem(at, sz.lc)
        n = jnp.where(there, by_k[base], 0)

        def pair(t, _):
            place = by_k[base + 1 + t]
            tile = lax.div(place, depth) * sz.lc + c
            late_list[2 + 2 * (total + t)] = h * (LR * depth) + place
            late_list[3 + 2 * (total + t)] = tile
            latest[tile] = total + t
            return 0

        lax.fori_loop(0, n, pair, 0)
        total = total + n

    def mark(t, tiles):
        tile = late_list[3 + 2 * t]
        last = (latest[tile] == t).astype(jnp.int32)
        late_list[3 + 2 * t] = 2 * tile + last
        return tiles + last

    late_list[0] = total
    late_list[1] = lax.fori_loop(0, total, mark, jnp.int32(0))


def tile(sz, i, c):
    return pl.ds(pl.multiple_of(i * sz.bs, sz.bs), sz.bs), pl.ds(pl.multiple_of(c * sz.bs, sz.bs), sz.bs)


def product_kernel(sz, starts, a_list, b_list, b_clear, a_sorted, *refs):
    b_refs, (total, out_ref, b_dense, sem) = refs[: len(starts)], refs[len(starts) :]
    bs, depth = sz.bs, sz.depth
    for start, b_ref in zip(starts, b_refs):
        for h in range(b_ref.shape[0] // bs):
            at = b_list[start + h]

            @pl.when(at >= 0)
            def _():
                k, c = lax.div(at, sz.lc), lax.rem(at, sz.lc)
                b_dense[k, :, pl.ds(pl.multiple_of(c * bs, bs), bs)] = b_ref[h * bs : (h + 1) * bs]

    width = total.shape[1]
    chunk = min(width, 512)

    def to_out(i):
        here = pl.ds(pl.multiple_of(i * bs, bs), bs)
        return pltpu.make_async_copy(total.at[here], out_ref.at[here], sem)

    def one_row(i, _):
        base = i * (depth + 1)
        n = a_list[base]
        here = pl.ds(pl.multiple_of(i * bs, bs), bs)

        def group(start, size, first):
            ks, blocks = [], []
            for t in range(size):
                at = jnp.minimum(start + t, depth - 1)
                there = start + t < n
                block = a_sorted[i * depth + at]
                blocks.append(jnp.where(there, block, jnp.zeros_like(block)))
                ks.append(jnp.where(there, a_list[base + 1 + at], 0))
            lhs = jnp.concatenate(blocks, axis=1)
            for c in range(0, width, chunk):
                rhs = jnp.concatenate([b_dense[k, :, c : c + chunk] for k in ks], axis=0)
                part = jnp.dot(lhs, rhs, preferred_element_type=jnp.float32)
                if first:
                    total[here, c : c + chunk] = part
                else:
                    total[here, c : c + chunk] += part

        @pl.when(n <= 2)
        def _():
            group(0, 2, True)

        @pl.when(n > 2)
        def _():
            group(0, 4, True)

        def more(g, _):
            group(4 + 2 * g, 2, False)
            return 0

        lax.fori_loop(0, lax.div(jnp.maximum(n - 3, 0), 2), more, 0)
        to_out(i).start()
        return 0

    lax.fori_loop(0, LR, one_row, 0)

    def done(i, _):
        to_out(i).wait()
        return 0

    lax.fori_loop(0, LR, done, 0)


def last_kernel(sz, late_list, total_in, out_in, a_sorted, *refs):
    b_refs, (total, out_ref, right, sem) = refs[:-4], refs[-4:]
    bs, every = sz.bs, LR * sz.depth
    count = late_list[0]
    at = 0
    for b_ref in b_refs:
        for h in range(b_ref.shape[0] // bs):
            right[at] = b_ref[h * bs : (h + 1) * bs]
            at += 1

    def to_out(at):
        return pltpu.make_async_copy(total.at[at], out_ref.at[at], sem)

    def place(t):
        code = late_list[3 + 2 * t]
        return tile(sz, lax.div(code, 2 * sz.lc), lax.rem(lax.div(code, 2), sz.lc)), lax.rem(code, 2) == 1

    def group(g, _):
        for u in range(AT_ONCE):
            t = g * AT_ONCE + u
            at = jnp.minimum(t, count - 1)
            code = late_list[2 + 2 * at]
            part = jnp.dot(
                a_sorted[lax.rem(code, every)], right[lax.div(code, every)], preferred_element_type=jnp.float32
            )
            total[place(at)[0]] += jnp.where(t < count, part, 0.0)
        for u in range(AT_ONCE):
            t = g * AT_ONCE + u
            at, last = place(jnp.minimum(t, count - 1))

            @pl.when((t < count) & last)
            def _():
                to_out(at).start()

        return 0

    lax.fori_loop(0, lax.div(count + AT_ONCE - 1, AT_ONCE), group, 0)

    def done(t, _):
        to_out((slice(0, bs), slice(0, bs))).wait()
        return 0

    lax.fori_loop(0, late_list[1], done, 0)


def flip(x, axis, d):
    return lax.ppermute(x, axis, [(i, i ^ d) for i in range(lax.axis_size(axis))])


def gather_by_flips(x, axis):
    n = lax.axis_size(axis)
    got, bit = {0: x}, n // 2
    while bit:
        for d in list(got):
            got[d | bit] = flip(got[d], axis, bit)
        bit //= 2
    return [got[d] for d in range(n)]


def per_device(x_tiles, tile_pos, panel_ids):
    rows, cols = lax.axis_size("row"), lax.axis_size("col")
    slots, bs, _ = x_tiles.shape
    dtype = x_tiles.dtype
    sz = Sizes(rows, cols, slots, bs)
    smem = pl.BlockSpec(memory_space=pltpu.SMEM)
    vmem = pl.BlockSpec(memory_space=pltpu.VMEM)

    *parts, mine, sections, plan = pl.pallas_call(
        functools.partial(pack_kernel, sz),
        out_shape=[pltpu.VMEM((sz.given(d) * bs + NOTE, bs), dtype) for d in range(rows)]
        + [
            pltpu.VMEM((slots * bs + NOTE, bs), dtype),
            pltpu.SMEM((sz.panels,), jnp.int32),
            pltpu.SMEM((3 * rows,), jnp.int32),
        ],
        in_specs=[smem, smem, vmem, vmem],
        out_specs=[vmem] * (rows + 1) + [smem, smem],
        scratch_shapes=[pltpu.SMEM((rows * 2 * sz.share,), jnp.int32)],
    )(tile_pos, panel_ids, tile_pos, x_tiles)

    in_vmem = functools.partial(pltpu.with_memory_space_constraint, memory_space=pltpu.VMEM)
    in_smem = functools.partial(pltpu.with_memory_space_constraint, memory_space=pltpu.SMEM)
    sections, plan = in_smem(sections), in_smem(plan)
    a_got, a_bit = {0: mine}, cols // 2
    a_got[a_bit] = flip(mine, "col", a_bit)
    came = [parts[0]]
    for d in range(1, rows):
        if d == rows - 2:
            parts[d], came[1] = lax.optimization_barrier((parts[d], came[1]))
        came.append(flip(parts[d], "row", d))
    hold, column_notes = pl.pallas_call(
        functools.partial(hold_kernel, sz),
        out_shape=[
            pltpu.VMEM((sz.held * bs, bs), dtype),
            jax.ShapeDtypeStruct((rows, slots), jnp.int32),
        ],
        in_specs=[smem] + [vmem] * rows,
        out_specs=[vmem, vmem],
    )(plan, *map(in_vmem, came))
    width = sz.lc * bs
    params = pltpu.CompilerParams(vmem_limit_bytes=32 * 2**20)
    b_list, b_clear = pl.pallas_call(
        functools.partial(column_meta_kernel, sz),
        out_shape=[
            pltpu.SMEM((rows * sz.held,), jnp.int32),
            pltpu.VMEM((sz.depth, bs, width), dtype),
        ],
        in_specs=[smem, smem, smem],
        out_specs=[smem, vmem],
        compiler_params=params,
    )(column_notes, sections, plan)

    bits = [1 << b for b in reversed(range(rows.bit_length() - 1))]
    a_got, hold_too = lax.optimization_barrier((a_got, hold))
    got = {0: [hold], **{bit: [flip(hold_too if bit < bits[0] else hold, "row", bit)] for bit in bits}}
    while a_bit:
        for d in list(a_got):
            if d | a_bit not in a_got:
                a_got[d | a_bit] = flip(a_got[d], "col", a_bit)
        a_bit //= 2
    a_parts = [a_got[d] for d in range(cols)]
    row_notes = jnp.stack([a[-1, :slots] for a in a_parts]).astype(jnp.int32)
    a_list, late_list, a_sorted = pl.pallas_call(
        functools.partial(row_meta_kernel, sz),
        out_shape=[
            pltpu.SMEM((LR * (sz.depth + 1),), jnp.int32),
            pltpu.SMEM((2 + 2 * len(sz.late) * LR,), jnp.int32),
            pltpu.VMEM((LR * sz.depth, bs, bs), dtype),
        ],
        in_specs=[smem] * 3 + [vmem] * cols,
        out_specs=[smem, smem, vmem],
        scratch_shapes=[
            pltpu.SMEM((sz.depth * (LR + 1),), jnp.int32),
            pltpu.SMEM((LR * sz.lc,), jnp.int32),
        ],
        compiler_params=params,
    )(row_notes, sections, in_smem(b_list), *map(in_vmem, a_parts))
    got[2], a_list, a_sorted = lax.optimization_barrier((got[2], a_list, a_sorted))
    if 3 not in got:
        got[3] = [flip(got[2][0], "row", 1)]
    (top, second), half = bits[:2], sz.held * bs // 2
    got[top], got[2], got[1], a_list, a_sorted = lax.optimization_barrier(
        (got[top], got[2], got[1], a_list, a_sorted)
    )
    first, rest = got[top][0][:half], got[top][0][half:]
    first, rest = flip(first, "row", second), flip(rest, "row", second)
    got[top | second] = [first, rest]
    got[top | second | 1] = [flip(p, "row", 1) for p in got[top | second]]
    after, _ = lax.optimization_barrier((got[1][0], first))
    got[top | 1] = [flip(got[top][0][:half], "row", 1), flip(after[half:], "row", top)]
    for bit in bits[1:]:
        for d in list(got):
            if d | bit not in got:
                got[d | bit] = [flip(p, "row", bit) for p in got[d]]

    early, late = [], []
    for d in range(rows):
        for i, piece in enumerate(got[d]):
            if d * sz.held in sz.late:
                late.append(in_vmem(piece))
            else:
                early.append((d * sz.held + i * half // bs, in_vmem(piece)))

    total, out = pl.pallas_call(
        functools.partial(product_kernel, sz, [start for start, _ in early]),
        out_shape=[
            pltpu.VMEM((LR * bs, width), jnp.float32),
            jax.ShapeDtypeStruct((LR * bs, width), jnp.float32),
            pltpu.VMEM((sz.depth, bs, width), dtype),
        ],
        in_specs=[smem, smem] + [vmem] * (2 + len(early)),
        out_specs=[vmem, pl.BlockSpec(memory_space=pl.ANY), vmem],
        input_output_aliases={2: 2},
        scratch_shapes=[pltpu.SemaphoreType.DMA],
        compiler_params=params,
        cost_estimate=pl.CostEstimate(flops=2 * 10**9, bytes_accessed=12 * 2**20, transcendentals=0),
    )(in_smem(a_list), in_smem(b_list), in_vmem(b_clear), in_vmem(a_sorted), *(b for _, b in early))[:2]
    return pl.pallas_call(
        functools.partial(last_kernel, sz),
        out_shape=[
            pltpu.VMEM((LR * bs, width), jnp.float32),
            jax.ShapeDtypeStruct((LR * bs, width), jnp.float32),
        ],
        in_specs=[smem, vmem, pl.BlockSpec(memory_space=pl.ANY), vmem] + [vmem] * len(late),
        out_specs=[vmem, pl.BlockSpec(memory_space=pl.ANY)],
        input_output_aliases={1: 0, 2: 1},
        scratch_shapes=[
            pltpu.VMEM((len(sz.late), bs, bs), dtype),
            pltpu.SemaphoreType.DMA,
        ],
        compiler_params=params,
    )(in_smem(late_list), in_vmem(total), out, in_vmem(a_sorted), *late)[1]


def solution(mesh):
    in_specs = (P("row", "col", None), P("row", "col"), P())
    out_specs = P("row", "col")
    return jax.shard_map(
        per_device, mesh=mesh, in_specs=in_specs, out_specs=out_specs, check_vma=False
    )
```

```python
import functools

import jax
import jax.numpy as jnp
from jax import lax
from jax.experimental import pallas as pl
from jax.experimental.pallas import tpu as pltpu
from jax.sharding import PartitionSpec as P

LR = 8
PW = 4
SECTIONS = 4
QD = 10
QS = 2
NOTE = 16
AT_ONCE = 12


class Sizes:
    def __init__(self, rows, cols, slots, bs):
        self.rows, self.cols, self.slots, self.bs = rows, cols, slots, bs
        self.lc = LR * rows // cols
        self.panels = rows * LR // PW
        panel_most = (self.lc // PW) * QS + (QD - QS)
        self.share = -(-panel_most // rows)
        self.near = -(-max(0, slots - rows * self.share) // self.share)
        self.held = SECTIONS * self.share
        self.depth = SECTIONS * PW
        self.late = [d * self.held + h for d in range(rows) if d & 1 and d & (rows // 2) for h in range(self.held)]

    def given(self, d):
        return self.share * (2 if d < self.near else 1)


def list_sections(sz, panels_ref, section_ref):
    for p in range(sz.panels):
        section_ref[p] = -1
    for j in range(SECTIONS):
        section_ref[panels_ref[j]] = j


def owned_by(panels_ref, row):
    count, first, last = jnp.int32(0), jnp.int32(-1), jnp.int32(0)
    for j in reversed(range(SECTIONS)):
        mine = lax.div(panels_ref[j], LR // PW) == row
        last = jnp.where(mine & (count == 0), j, last)
        first = jnp.where(mine, j, first)
        count = count + mine.astype(jnp.int32)
    return count, first, last


def deal(sz, count, picked, e, i):
    i = jnp.where(picked, i + 1, i)
    full = i == jnp.where((count == 2) & (e < sz.near), 2 * sz.share, sz.share)
    return jnp.where(full, e + 1, e), jnp.where(full, 0, i)


def pack_kernel(sz, pos_ref, panels_ref, pos_row_ref, x_ref, *refs):
    outs, (all_ref, section_ref, plan_ref, src_ref) = refs[: sz.rows], refs[sz.rows :]
    row = lax.axis_index("row")
    count, _, _ = owned_by(panels_ref, row)
    bs, most = sz.bs, 2 * sz.share
    for e in range(sz.rows * most):
        src_ref[e] = 0
    list_sections(sz, panels_ref, section_ref)
    for d in range(sz.rows):
        for i, value in enumerate(owned_by(panels_ref, row ^ d)):
            plan_ref[3 * d + i] = value

    e, i = jnp.int32(0), jnp.int32(0)
    for s in range(sz.slots):
        picked = section_ref[row * (LR // PW) + lax.div(pos_ref[0, s], sz.lc * PW)] >= 0

        @pl.when(picked)
        def _():
            src_ref[e * most + i] = s

        e, i = deal(sz, count, picked, e, i)
    note = jnp.broadcast_to(pos_row_ref[...].astype(jnp.float32), (NOTE, sz.slots)).astype(x_ref.dtype)
    for e in range(sz.rows):
        for i in range(sz.given(e)):
            outs[e][i * bs : (i + 1) * bs] = x_ref[src_ref[e * most + i]]
        outs[e][sz.given(e) * bs :, : sz.slots] = note
    for s in range(sz.slots):
        all_ref[s * bs : (s + 1) * bs] = x_ref[s]
    all_ref[sz.slots * bs :, : sz.slots] = note


def hold_kernel(sz, plan_ref, *refs):
    came, hold_ref, notes_ref = refs[: sz.rows], refs[sz.rows], refs[sz.rows + 1]
    n = sz.share * sz.bs

    for d in range(sz.rows):
        note = came[d][sz.given(d) * sz.bs :].astype(jnp.float32)[:1, : sz.slots]
        notes_ref[d : d + 1, :] = note.astype(jnp.int32)
    for d in range(sz.rows):
        count, first, last = (plan_ref[3 * d + i] for i in range(3))

        @pl.when(count > 0)
        def _():
            hold_ref[pl.ds(pl.multiple_of(first * n, n), n)] = came[d][:n]

        if d < sz.near:

            @pl.when(count == 2)
            def _():
                hold_ref[pl.ds(pl.multiple_of(last * n, n), n)] = came[d][n : 2 * n]


def column_meta_kernel(sz, notes_ref, section_ref, plan_ref, b_list, b_dense):
    row = lax.axis_index("row")
    b_dense[...] = jnp.zeros_like(b_dense)

    for i in range(sz.rows * sz.held):
        b_list[i] = -1

    def one_row(d, _):
        count, first, last = (plan_ref[3 * d + i] for i in range(3))
        owner = row ^ d

        def one(s, state):
            e, i = state
            pos = notes_ref[d, s]
            local_row, local_col = lax.div(pos, sz.lc), lax.rem(pos, sz.lc)
            section = section_ref[owner * (LR // PW) + lax.div(local_row, PW)]
            picked = section >= 0

            @pl.when(picked)
            def _():
                at = jnp.where(i < sz.share, first * sz.share + i, last * sz.share + i - sz.share)
                b_list[(d ^ e) * sz.held + at] = (section * PW + lax.rem(local_row, PW)) * sz.lc + local_col

            return deal(sz, count, picked, e, i)

        @pl.when(count > 0)
        def _():
            lax.fori_loop(0, sz.slots, one, (jnp.int32(0), jnp.int32(0)))

        return 0

    lax.fori_loop(0, sz.rows, one_row, 0)


def row_meta_kernel(sz, notes_ref, section_ref, b_list, *refs):
    a_refs, (a_list, late_list, a_sorted, by_k, latest) = refs[: sz.cols], refs[sz.cols :]
    col = lax.axis_index("col")
    bs, depth = sz.bs, sz.depth
    for i in range(LR):
        a_list[i * (depth + 1)] = 0
    for k in range(depth):
        by_k[k * (LR + 1)] = 0

    for e in range(sz.cols):

        def one(s, _):
            pos = notes_ref[e, s]
            local_row, local_col = lax.div(pos, sz.lc), lax.rem(pos, sz.lc)
            section = section_ref[(e ^ col) * (sz.lc // PW) + lax.div(local_col, PW)]

            @pl.when(section >= 0)
            def _():
                k = section * PW + lax.rem(local_col, PW)
                base = local_row * (depth + 1)
                n = a_list[base]
                a_list[base + 1 + n] = k
                a_list[base] = n + 1
                place = local_row * depth + n
                base = k * (LR + 1)
                n = by_k[base]
                by_k[base + 1 + n] = place
                by_k[base] = n + 1
                a_sorted[place] = a_refs[e][pl.ds(pl.multiple_of(s * bs, bs), bs), :]

            return 0

        lax.fori_loop(0, sz.slots, one, 0)

    total = jnp.int32(0)
    for h, at_place in enumerate(sz.late):
        at = b_list[at_place]
        there = at >= 0
        at = jnp.maximum(at, 0)
        base, c = lax.div(at, sz.lc) * (LR + 1), lax.rem(at, sz.lc)
        n = jnp.where(there, by_k[base], 0)

        def pair(t, _):
            place = by_k[base + 1 + t]
            tile = lax.div(place, depth) * sz.lc + c
            late_list[2 + 2 * (total + t)] = h * (LR * depth) + place
            late_list[3 + 2 * (total + t)] = tile
            latest[tile] = total + t
            return 0

        lax.fori_loop(0, n, pair, 0)
        total = total + n

    def mark(t, tiles):
        tile = late_list[3 + 2 * t]
        last = (latest[tile] == t).astype(jnp.int32)
        late_list[3 + 2 * t] = 2 * tile + last
        return tiles + last

    late_list[0] = total
    late_list[1] = lax.fori_loop(0, total, mark, jnp.int32(0))


def tile(sz, i, c):
    return pl.ds(pl.multiple_of(i * sz.bs, sz.bs), sz.bs), pl.ds(pl.multiple_of(c * sz.bs, sz.bs), sz.bs)


def product_kernel(sz, starts, a_list, b_list, b_clear, a_sorted, *refs):
    b_refs, (total, out_ref, b_dense, sem) = refs[: len(starts)], refs[len(starts) :]
    bs, depth = sz.bs, sz.depth
    for start, b_ref in zip(starts, b_refs):
        for h in range(b_ref.shape[0] // bs):
            at = b_list[start + h]

            @pl.when(at >= 0)
            def _():
                k, c = lax.div(at, sz.lc), lax.rem(at, sz.lc)
                b_dense[k, :, pl.ds(pl.multiple_of(c * bs, bs), bs)] = b_ref[h * bs : (h + 1) * bs]

    width = total.shape[1]
    chunk = min(width, 512)

    def to_out(i):
        here = pl.ds(pl.multiple_of(i * bs, bs), bs)
        return pltpu.make_async_copy(total.at[here], out_ref.at[here], sem)

    def one_row(i, _):
        base = i * (depth + 1)
        n = a_list[base]
        here = pl.ds(pl.multiple_of(i * bs, bs), bs)

        def group(start, size, first):
            ks, blocks = [], []
            for t in range(size):
                at = jnp.minimum(start + t, depth - 1)
                there = start + t < n
                block = a_sorted[i * depth + at]
                blocks.append(jnp.where(there, block, jnp.zeros_like(block)))
                ks.append(jnp.where(there, a_list[base + 1 + at], 0))
            lhs = jnp.concatenate(blocks, axis=1)
            for c in range(0, width, chunk):
                rhs = jnp.concatenate([b_dense[k, :, c : c + chunk] for k in ks], axis=0)
                part = jnp.dot(lhs, rhs, preferred_element_type=jnp.float32)
                if first:
                    total[here, c : c + chunk] = part
                else:
                    total[here, c : c + chunk] += part

        @pl.when(n <= 2)
        def _():
            group(0, 2, True)

        @pl.when(n > 2)
        def _():
            group(0, 4, True)

        def more(g, _):
            group(4 + 2 * g, 2, False)
            return 0

        lax.fori_loop(0, lax.div(jnp.maximum(n - 3, 0), 2), more, 0)
        to_out(i).start()
        return 0

    lax.fori_loop(0, LR, one_row, 0)

    def done(i, _):
        to_out(i).wait()
        return 0

    lax.fori_loop(0, LR, done, 0)


def last_kernel(sz, late_list, total_in, out_in, a_sorted, *refs):
    b_refs, (total, out_ref, right, sem) = refs[:-4], refs[-4:]
    bs, every = sz.bs, LR * sz.depth
    count = late_list[0]
    at = 0
    for b_ref in b_refs:
        for h in range(b_ref.shape[0] // bs):
            right[at] = b_ref[h * bs : (h + 1) * bs]
            at += 1

    def to_out(at):
        return pltpu.make_async_copy(total.at[at], out_ref.at[at], sem)

    def place(t):
        code = late_list[3 + 2 * t]
        return tile(sz, lax.div(code, 2 * sz.lc), lax.rem(lax.div(code, 2), sz.lc)), lax.rem(code, 2) == 1

    def group(g, _):
        for u in range(AT_ONCE):
            t = g * AT_ONCE + u
            at = jnp.minimum(t, count - 1)
            code = late_list[2 + 2 * at]
            part = jnp.dot(
                a_sorted[lax.rem(code, every)], right[lax.div(code, every)], preferred_element_type=jnp.float32
            )
            total[place(at)[0]] += jnp.where(t < count, part, 0.0)
        for u in range(AT_ONCE):
            t = g * AT_ONCE + u
            at, last = place(jnp.minimum(t, count - 1))

            @pl.when((t < count) & last)
            def _():
                to_out(at).start()

        return 0

    lax.fori_loop(0, lax.div(count + AT_ONCE - 1, AT_ONCE), group, 0)

    def done(t, _):
        to_out((slice(0, bs), slice(0, bs))).wait()
        return 0

    lax.fori_loop(0, late_list[1], done, 0)


def flip(x, axis, d):
    return lax.ppermute(x, axis, [(i, i ^ d) for i in range(lax.axis_size(axis))])


def gather_by_flips(x, axis):
    n = lax.axis_size(axis)
    got, bit = {0: x}, n // 2
    while bit:
        for d in list(got):
            got[d | bit] = flip(got[d], axis, bit)
        bit //= 2
    return [got[d] for d in range(n)]


def per_device(x_tiles, tile_pos, panel_ids):
    rows, cols = lax.axis_size("row"), lax.axis_size("col")
    slots, bs, _ = x_tiles.shape
    dtype = x_tiles.dtype
    sz = Sizes(rows, cols, slots, bs)
    smem = pl.BlockSpec(memory_space=pltpu.SMEM)
    vmem = pl.BlockSpec(memory_space=pltpu.VMEM)

    *parts, mine, sections, plan = pl.pallas_call(
        functools.partial(pack_kernel, sz),
        out_shape=[pltpu.VMEM((sz.given(d) * bs + NOTE, bs), dtype) for d in range(rows)]
        + [
            pltpu.VMEM((slots * bs + NOTE, bs), dtype),
            pltpu.SMEM((sz.panels,), jnp.int32),
            pltpu.SMEM((3 * rows,), jnp.int32),
        ],
        in_specs=[smem, smem, vmem, vmem],
        out_specs=[vmem] * (rows + 1) + [smem, smem],
        scratch_shapes=[pltpu.SMEM((rows * 2 * sz.share,), jnp.int32)],
    )(tile_pos, panel_ids, tile_pos, x_tiles)

    in_vmem = functools.partial(pltpu.with_memory_space_constraint, memory_space=pltpu.VMEM)
    in_smem = functools.partial(pltpu.with_memory_space_constraint, memory_space=pltpu.SMEM)
    sections, plan = in_smem(sections), in_smem(plan)
    a_got, a_bit = {0: mine}, cols // 2
    a_got[a_bit] = flip(mine, "col", a_bit)
    came = [parts[0]]
    for d in range(1, rows):
        if d == rows - 2:
            parts[d], came[1] = lax.optimization_barrier((parts[d], came[1]))
        came.append(flip(parts[d], "row", d))
    hold, column_notes = pl.pallas_call(
        functools.partial(hold_kernel, sz),
        out_shape=[
            pltpu.VMEM((sz.held * bs, bs), dtype),
            jax.ShapeDtypeStruct((rows, slots), jnp.int32),
        ],
        in_specs=[smem] + [vmem] * rows,
        out_specs=[vmem, vmem],
    )(plan, *map(in_vmem, came))
    width = sz.lc * bs
    params = pltpu.CompilerParams(vmem_limit_bytes=32 * 2**20)
    b_list, b_clear = pl.pallas_call(
        functools.partial(column_meta_kernel, sz),
        out_shape=[
            pltpu.SMEM((rows * sz.held,), jnp.int32),
            pltpu.VMEM((sz.depth, bs, width), dtype),
        ],
        in_specs=[smem, smem, smem],
        out_specs=[smem, vmem],
        compiler_params=params,
    )(column_notes, sections, plan)

    bits = [1 << b for b in reversed(range(rows.bit_length() - 1))]
    a_got, hold_too = lax.optimization_barrier((a_got, hold))
    got = {0: [hold], **{bit: [flip(hold_too if bit < bits[0] else hold, "row", bit)] for bit in bits}}
    while a_bit:
        for d in list(a_got):
            if d | a_bit not in a_got:
                a_got[d | a_bit] = flip(a_got[d], "col", a_bit)
        a_bit //= 2
    a_parts = [a_got[d] for d in range(cols)]
    row_notes = jnp.stack([a[-1, :slots] for a in a_parts]).astype(jnp.int32)
    a_list, late_list, a_sorted = pl.pallas_call(
        functools.partial(row_meta_kernel, sz),
        out_shape=[
            pltpu.SMEM((LR * (sz.depth + 1),), jnp.int32),
            pltpu.SMEM((2 + 2 * len(sz.late) * LR,), jnp.int32),
            pltpu.VMEM((LR * sz.depth, bs, bs), dtype),
        ],
        in_specs=[smem] * 3 + [vmem] * cols,
        out_specs=[smem, smem, vmem],
        scratch_shapes=[
            pltpu.SMEM((sz.depth * (LR + 1),), jnp.int32),
            pltpu.SMEM((LR * sz.lc,), jnp.int32),
        ],
        compiler_params=params,
    )(row_notes, sections, in_smem(b_list), *map(in_vmem, a_parts))
    got[2], a_list, a_sorted = lax.optimization_barrier((got[2], a_list, a_sorted))
    if 3 not in got:
        got[3] = [flip(got[2][0], "row", 1)]
    (top, second), half = bits[:2], sz.held * bs // 2
    got[top], got[2], got[1], a_list, a_sorted = lax.optimization_barrier(
        (got[top], got[2], got[1], a_list, a_sorted)
    )
    first, rest = got[top][0][:half], got[top][0][half:]
    first, rest = flip(first, "row", second), flip(rest, "row", second)
    got[top | second] = [first, rest]
    got[top | second | 1] = [flip(p, "row", 1) for p in got[top | second]]
    got[top | 1] = [flip(got[top][0][:half], "row", 1), flip(got[1][0][half:], "row", top)]
    for bit in bits[1:]:
        for d in list(got):
            if d | bit not in got:
                got[d | bit] = [flip(p, "row", bit) for p in got[d]]

    early, late = [], []
    for d in range(rows):
        for i, piece in enumerate(got[d]):
            if d * sz.held in sz.late:
                late.append(in_vmem(piece))
            else:
                early.append((d * sz.held + i * half // bs, in_vmem(piece)))

    total, out = pl.pallas_call(
        functools.partial(product_kernel, sz, [start for start, _ in early]),
        out_shape=[
            pltpu.VMEM((LR * bs, width), jnp.float32),
            jax.ShapeDtypeStruct((LR * bs, width), jnp.float32),
            pltpu.VMEM((sz.depth, bs, width), dtype),
        ],
        in_specs=[smem, smem] + [vmem] * (2 + len(early)),
        out_specs=[vmem, pl.BlockSpec(memory_space=pl.ANY), vmem],
        input_output_aliases={2: 2},
        scratch_shapes=[pltpu.SemaphoreType.DMA],
        compiler_params=params,
        cost_estimate=pl.CostEstimate(flops=2 * 10**9, bytes_accessed=12 * 2**20, transcendentals=0),
    )(in_smem(a_list), in_smem(b_list), in_vmem(b_clear), in_vmem(a_sorted), *(b for _, b in early))[:2]
    return pl.pallas_call(
        functools.partial(last_kernel, sz),
        out_shape=[
            pltpu.VMEM((LR * bs, width), jnp.float32),
            jax.ShapeDtypeStruct((LR * bs, width), jnp.float32),
        ],
        in_specs=[smem, vmem, pl.BlockSpec(memory_space=pl.ANY), vmem] + [vmem] * len(late),
        out_specs=[vmem, pl.BlockSpec(memory_space=pl.ANY)],
        input_output_aliases={1: 0, 2: 1},
        scratch_shapes=[
            pltpu.VMEM((len(sz.late), bs, bs), dtype),
            pltpu.SemaphoreType.DMA,
        ],
        compiler_params=params,
    )(in_smem(late_list), in_vmem(total), out, in_vmem(a_sorted), *late)[1]


def solution(mesh):
    in_specs = (P("row", "col", None), P("row", "col"), P())
    out_specs = P("row", "col")
    return jax.shard_map(
        per_device, mesh=mesh, in_specs=in_specs, out_specs=out_specs, check_vma=False
    )
```
